256 devices in a mesh: dp: 2 (over x_hi), ctx: 32 (over z, x_lo, core), tensor: 4 (over y).
Axes of the slice: x: 4 (x_hi: 2, x_lo: 2; x = x_hi * 2 + x_lo), y: 4, z: 8, core: 2. Of those that a mesh axis runs over, the one named last changes fastest.
Arguments:
- queries: bfloat16 [4096, 2, 32, 128], P('ctx', 'dp', 'tensor'), may hold values from -200 to 200
- keys: bfloat16 [4096, 2, 4, 128], P('ctx', 'dp', 'tensor'), may hold values from -6 to 6
- values: bfloat16 [4096, 2, 4, 128], P('ctx', 'dp', 'tensor'), may hold values from -6 to 6
- segment_ids: int32 [64], P('ctx'), may hold values from 0 to 63, as said below
- feat_query: bfloat16 [32, 128, 64], P('tensor'), may hold values from -0.5 to 0.5
- feat_key: bfloat16 [32, 128, 64], P('tensor'), may hold values from -0.5 to 0.5
Outputs:
- student: bfloat16 [4096, 2, 32, 128], P('ctx', 'dp', 'tensor')
- grad_query: float32 [32, 128, 64], P('tensor')
- grad_key: float32 [32, 128, 64], P('tensor')
The draws below stay inside these ranges and needn't reach their ends.
Inputs may be any that keep to these rules, and one draw needn't show every extreme that they name: `segment_ids`: entries 2 i and 2 i + 1 are the numbers i and 63 - i, in either order.
All inputs are finite; a program needn't handle non-finite values.
Results may differ from the reference program's by a relative error of at most 0.007.
Values may be sent and summed in bfloat16 or wider, within the bound.
No kernel may reach another device: no remote copies, remote signals or barrier semaphores. Data moves between devices by JAX's collectives and lax.ppermute only.
A program may use at most 128 MiB of HBM per device.

```python
import math
import jax
import jax.numpy as jnp
from jax import lax

QH = 32
KVH = 4
HD = 128
FD = 64
SEGMENT = 64
NSEG = 64
LEN = 4096
SEQS = 2


def shared_keys(key):
    return jnp.clip(jax.random.normal(key, (LEN, SEQS, KVH, HD), jnp.float32), -6.0, 6.0)


def draw_keys(key, part):
    base_keys = shared_keys(key)
    return base_keys.astype(jnp.bfloat16)


def draw_queries(key, part):
    key = jax.random.fold_in(key, 11)
    drawn_rows = jnp.clip(jax.random.normal(key, (LEN, SEQS, QH, HD), jnp.float32), -6.0, 6.0)
    return drawn_rows.astype(jnp.bfloat16)


def draw_segment_ids(key, part):
    key = jax.random.fold_in(key, 29)
    pair_count = NSEG // 2
    lower_ids = jnp.arange(pair_count, dtype=jnp.int32)
    upper_ids = NSEG - 1 - lower_ids
    flip_bits = (jax.random.bits(key, (pair_count,), jnp.uint32) >> 7).astype(jnp.int32) % 2
    first_ids = jnp.where(flip_bits == 1, upper_ids, lower_ids)
    second_ids = jnp.where(flip_bits == 1, lower_ids, upper_ids)
    return jnp.stack([first_ids, second_ids], axis=1).reshape(NSEG)


def level_of(rng, shape, shards, low, largest):
    gain, own = 1.0, jax.random.fold_in(rng, 6)
    for axis_at, parts in shards:
        draws = jnp.exp(jax.random.uniform(jax.random.fold_in(own, axis_at), (parts,), jnp.float32, low / len(shards), largest / len(shards)))
        gain = gain * jnp.repeat(draws, shape[axis_at] // parts).reshape([-1 if axis == axis_at else 1 for axis in range(len(shape))])
    return gain


def scatter_about(own_key, dims, width, limit, cuts=(), held_as=jnp.bfloat16):
    entries = width * jax.random.normal(own_key, dims, jnp.float32)
    if cuts:
        entries = entries * level_of(own_key, dims, cuts, -0.22, 0.18)
    return jnp.clip(entries, -limit, limit).astype(held_as)


def setup_inputs(seed: int = 0) -> dict:
    splits = jax.random.split(jax.random.key(seed), 7)
    queries = draw_queries(jax.random.fold_in(splits[6], 71), 0)
    keys = draw_keys(jax.random.fold_in(splits[6], 71), 0)
    values = scatter_about(splits[2], (LEN, SEQS, KVH, HD), 1.0, 6.0, ((0, 32), (1, 2), (2, 4)))
    segment_ids = draw_segment_ids(jax.random.fold_in(splits[6], 71), 0)
    feat_query = scatter_about(splits[4], (QH, HD, FD), HD ** -0.5, 0.5, ((0, 4),))
    feat_key = scatter_about(splits[5], (QH, HD, FD), HD ** -0.5, 0.5, ((0, 4),))
    return dict(queries=queries, keys=keys, values=values, segment_ids=segment_ids, feat_query=feat_query, feat_key=feat_key)


NEGATIVE = -1e+30
EXACT = lax.Precision.HIGHEST

def feature_map(inputs, weight):
    projected = jnp.einsum('thd,hdf->thf', inputs, weight, precision=EXACT)
    return jnp.concatenate([jax.nn.softmax(projected, axis=-1), jax.nn.softmax(-projected, axis=-1)], axis=-1)

def widen(inputs, head_count):
    return jnp.repeat(inputs, head_count // inputs.shape[1], axis=1)

def segment_states(phi_keys, value_rows):
    states = jnp.einsum('cthf,cthd->chfd', phi_keys, value_rows, precision=EXACT)
    return (states, lax.optimization_barrier(jnp.sum(phi_keys, axis=1)))

def segment_output(phi_queries, phi_keys, value_rows, prior_states, prior_sums):
    block_width = phi_queries.shape[1]
    causal = jnp.arange(block_width)[None, :] <= jnp.arange(block_width)[:, None]
    numerator = jnp.einsum('cthf,chfd->cthd', phi_queries, prior_states, precision=EXACT)
    denominator = jnp.einsum('cthf,chf->cth', phi_queries, prior_sums, precision=EXACT)
    weights = jnp.einsum('cthf,cshf->chts', phi_queries, phi_keys, precision=EXACT)
    weights = jnp.where(causal[None, None], weights, 0.0)
    numerator = numerator + jnp.einsum('chts,cshd->cthd', weights, value_rows, precision=EXACT)
    denominator = denominator + jnp.transpose(lax.optimization_barrier(jnp.sum(weights, axis=3)), (0, 2, 1))
    return numerator / denominator[..., None]

def teacher_head(query_head, key_head, value_head):
    block_rows = math.gcd(LEN, 512)
    score_scale = HD ** (-0.5)
    key_positions = jnp.arange(LEN, dtype=jnp.int32)

    def one_block(first_row):
        query_rows = lax.dynamic_slice_in_dim(query_head, first_row, block_rows, 0)
        query_positions = first_row + jnp.arange(block_rows, dtype=jnp.int32)
        scores = jnp.dot(query_rows, key_head.T, precision=EXACT) * score_scale
        causal = key_positions[None, :] <= query_positions[:, None]
        row_top = lax.optimization_barrier(jnp.max(jnp.where(causal, scores, NEGATIVE), axis=1, keepdims=True))
        weights = jnp.where(causal, jnp.exp(scores - row_top), 0.0)
        total = lax.optimization_barrier(jnp.sum(weights, axis=1, keepdims=True))
        rounded = lax.optimization_barrier(weights.astype(jnp.bfloat16)).astype(jnp.float32)
        return jnp.dot(rounded, value_head, precision=EXACT) / total
    starts = jnp.arange(LEN // block_rows, dtype=jnp.int32) * block_rows
    return lax.map(one_block, starts).reshape(LEN, value_head.shape[1])

def reference(queries, keys, values, segment_ids, feat_query, feat_key):

    def natural(array):
        pieces = array.reshape((NSEG, SEGMENT) + array.shape[1:])
        return jnp.zeros_like(pieces).at[segment_ids].set(pieces).reshape(array.shape)

    def stored(array):
        pieces = array.reshape((NSEG, SEGMENT) + array.shape[1:])
        return pieces[segment_ids].reshape(array.shape)
    query_all = natural(queries).astype(jnp.float32)
    key_all = natural(keys).astype(jnp.float32)
    value_all = natural(values).astype(jnp.float32)
    weight_query = feat_query.astype(jnp.float32)
    weight_key = feat_key.astype(jnp.float32)
    group_size = QH // KVH
    outputs = []
    grad_query = jnp.zeros(weight_query.shape, jnp.float32)
    grad_key = jnp.zeros(weight_key.shape, jnp.float32)
    for seq_index in range(SEQS):
        query_rows = query_all[:, seq_index]
        key_rows = key_all[:, seq_index]
        value_rows = value_all[:, seq_index]
        head_queries = jnp.transpose(query_rows, (1, 0, 2))
        head_keys = jnp.repeat(jnp.transpose(key_rows, (1, 0, 2)), group_size, axis=0)
        head_values = jnp.repeat(jnp.transpose(value_rows, (1, 0, 2)), group_size, axis=0)
        teacher = lax.map(lambda triple: teacher_head(triple[0], triple[1], triple[2]), (head_queries, head_keys, head_values))
        teacher = jnp.transpose(teacher, (1, 0, 2))
        wide_values = widen(value_rows, QH).reshape(NSEG, SEGMENT, QH, HD)

        def student_of(weight_one, weight_two):
            phi_queries = feature_map(query_rows, weight_one).reshape(NSEG, SEGMENT, QH, 2 * FD)
            phi_keys = feature_map(widen(key_rows, QH), weight_two).reshape(NSEG, SEGMENT, QH, 2 * FD)
            states, sums = segment_states(phi_keys, wide_values)
            prior_states = jnp.cumsum(states, axis=0) - states
            prior_sums = jnp.cumsum(sums, axis=0) - sums
            result = segment_output(phi_queries, phi_keys, wide_values, prior_states, prior_sums)
            return result.reshape(LEN, QH, HD)
        student, student_back = jax.vjp(student_of, weight_query, weight_key)
        cotangent = (student - teacher) / (LEN * SEQS)
        more_query, more_key = student_back(cotangent)
        grad_query = grad_query + more_query
        grad_key = grad_key + more_key
        outputs.append(student)
    student_all = stored(jnp.stack(outputs, axis=1))
    return (student_all.astype(jnp.bfloat16), grad_query, grad_key)
```

```python
import math

import jax
import jax.numpy as jnp
from jax import lax
from jax.experimental import pallas as pl
from jax.experimental.pallas import tpu as pltpu
from jax.sharding import PartitionSpec as P

PLACES = 8
MEMBERS = 4
SEG = 64
HD = 128
FD = 64
PHI = 2 * FD
BLOCKS = 4
ROWS = 4 * SEG
HALF = 8 * SEG
AUG = HD + 16
LOSS = 1.0 / 8192.0
F32 = jnp.float32
BF16 = jnp.bfloat16
NN = (((1,), (0,)), ((), ()))
NT = (((1,), (1,)), ((), ()))


def dot(a, b, dims=NN):
    return lax.dot_general(a, b, dims, preferred_element_type=F32)


def split(array):
    high = array.astype(BF16)
    return high, (array - high.astype(F32)).astype(BF16)


def causal_mask(member, others, late):
    def turn(who):
        return 3 - who if late else who

    key = lax.broadcasted_iota(jnp.int32, (HALF, 1), 0)
    row = lax.broadcasted_iota(jnp.int32, (1, ROWS), 1)
    second = (key // SEG) % 2
    who = jnp.where(second == 0, member ^ others[0], member ^ others[1])
    key_at = (key // (2 * SEG)) * (4 * SEG) + turn(who) * SEG + key % SEG
    row_at = (row // SEG) * (4 * SEG) + turn(member) * SEG + row % SEG
    return key_at <= row_at


def features(projected):
    top = jnp.max(projected, axis=0, keepdims=True)
    bottom = jnp.min(projected, axis=0, keepdims=True)
    plus = jnp.exp(projected - top)
    minus = jnp.exp(bottom - projected)
    plus = plus * (1.0 / jnp.sum(plus, axis=0, keepdims=True))
    minus = minus * (1.0 / jnp.sum(minus, axis=0, keepdims=True))
    return jnp.concatenate([plus, minus], axis=0)


def features_back(phi, grad):
    term = phi * grad
    plus, minus = term[:FD], term[FD:]
    plus = plus - phi[:FD] * jnp.sum(plus, axis=0, keepdims=True)
    minus = minus - phi[FD:] * jnp.sum(minus, axis=0, keepdims=True)
    return plus - minus


def where_is(chunk):
    return (chunk, 0) if chunk < PLACES else (2 * PLACES - 1 - chunk, 1)


def block_rows(refs, block, columns):
    rows = []
    for chunk in range(4 * block, 4 * block + 4):
        place, late = where_is(chunk)
        rows += [ref[place, late, :, columns] for ref in refs]
    return jnp.concatenate(rows, axis=0)


KEY = slice(0, HD)
VALUE = slice(HD, 2 * HD)
QUERY = slice(2 * HD, 3 * HD)


def pack_kernel(ids_ref, q_ref, k_ref, v_ref, out_ref, wide):
    wide[...] = q_ref[...].astype(F32)
    swapped = ids_ref[0] > ids_ref[1]
    for late in range(2):
        start = jnp.where(swapped, SEG - SEG * late, SEG * late)
        rows = pl.ds(pl.multiple_of(start, SEG), SEG)
        pair = jnp.concatenate([k_ref[rows], v_ref[rows]], axis=1)
        for place in range(PLACES):
            out_ref[place, late, :, :2 * HD] = pair
            head = wide[pl.ds(start * PLACES + place, SEG, stride=PLACES)]
            out_ref[place, late, :, 2 * HD:] = head.astype(BF16)


def half_forward(refs, masks, queries, phi_q, wk, outs):
    top_ref, total_ref, acc_ref, num_ref, state_ref, phik_ref = outs
    scale = (HD ** -0.5) * math.log2(math.e)
    keys, values_t = [], []
    for block in range(BLOCKS):
        keys.append(block_rows(refs, block, KEY))
        value = block_rows(refs, block, VALUE).T
        values_t.append(jnp.concatenate([value, jnp.ones((AUG - HD, HALF), BF16)], axis=0))
    for block in range(BLOCKS):
        phi = features(dot(wk, keys[block], NT))
        phik_ref[block] = phi
        high, low = split(phi)
        state_ref[block] = dot(values_t[block], high, NT) + dot(values_t[block], low, NT)
        pair = dot(high.T, phi_q[block])
        high, low = split(jnp.where(masks[block // 2], pair, 0.0))
        num_ref[block] = dot(values_t[block], high) + dot(values_t[block], low)

        scores = [dot(keys[b], queries[block], NT) for b in range(block + 1)]
        scores[-1] = jnp.where(masks[block // 2], scores[-1], -1e30)
        top = jnp.max(scores[0], axis=0, keepdims=True)
        for s in scores[1:]:
            top = jnp.maximum(top, jnp.max(s, axis=0, keepdims=True))
        total, acc = 0.0, 0.0
        for b, s in enumerate(scores):
            weights = jnp.exp2(s * scale - top * scale)
            total = total + jnp.sum(weights, axis=0, keepdims=True)
            acc = acc + dot(values_t[b][:HD], weights.astype(BF16))
        top_ref[block] = top * scale
        total_ref[block] = total
        acc_ref[block] = acc


def first_kernel(at_ref, own_ref, core_ref, wq_ref, wk_ref, phiq_ref, *outs):
    place, member = at_ref[0], at_ref[1]
    masks = [causal_mask(member, (0, 1), late) for late in (False, True)]
    queries = [block_rows((own_ref,), b, QUERY) for b in range(BLOCKS)]
    phi_q = []
    for block in range(BLOCKS):
        phi = features(dot(wq_ref[place], queries[block], NT))
        phiq_ref[block] = phi
        phi_q.append(phi.astype(BF16))
    half_forward((own_ref, core_ref), masks, queries, phi_q, wk_ref[place], outs)


def second_kernel(
    at_ref, own_ref, x_ref, far_ref, wk_ref, phiq_ref,
    top_ref, total_ref, acc_ref, num_ref, state_ref,
    student_ref, phik_ref, prior_ref, dn_ref,
    top2_ref, total2_ref, acc2_ref, num2_ref, state2_ref,
):
    place, member = at_ref[0], at_ref[1]
    masks = [causal_mask(member, (2, 3), late) for late in (False, True)]
    queries = [block_rows((own_ref,), b, QUERY) for b in range(BLOCKS)]
    phi_q = [phiq_ref[block].astype(BF16) for block in range(BLOCKS)]
    outs = (top2_ref, total2_ref, acc2_ref, num2_ref, state2_ref, phik_ref)
    half_forward((x_ref, far_ref), masks, queries, phi_q, wk_ref[place], outs)
    prior = jnp.zeros((AUG, PHI), F32)
    for block in range(BLOCKS):
        top = jnp.maximum(top_ref[block], top2_ref[block])
        one = jnp.exp2(top_ref[block] - top)
        two = jnp.exp2(top2_ref[block] - top)
        total = total_ref[block] * one + total2_ref[block] * two
        teacher = (acc_ref[block] * one + acc2_ref[block] * two) * (1.0 / total)
        prior_ref[block] = prior
        numerator = num_ref[block] + num2_ref[block]
        if block > 0:
            high, low = split(prior)
            numerator = numerator + dot(
                jnp.concatenate([high, low], axis=1),
                jnp.concatenate([phi_q[block]] * 2, axis=0),
            )
        prior = prior + state_ref[block] + state2_ref[block]
        inverse = 1.0 / numerator[HD:HD + 1]
        y = numerator[:HD] * inverse
        d_num = (y - teacher) * (inverse * LOSS)
        d_den = -jnp.sum(d_num * y, axis=0, keepdims=True)
        high, low = split(d_num)
        den_high, den_low = split(d_den)
        index = lax.broadcasted_iota(jnp.int32, (AUG - HD, ROWS), 0)
        extra = jnp.where(
            index == 0, den_high.astype(F32), jnp.where(index == 1, den_low.astype(F32), 0.0)
        )
        dn_ref[block] = jnp.concatenate([high, low, extra.astype(BF16)], axis=0)
        rows = y.T.astype(BF16)
        for i in range(4):
            place, late = where_is(4 * block + i)
            student_ref[place, late] = rows[i * SEG:(i + 1) * SEG]


def backward_kernel(
    at_ref, own_ref, core_ref, x_ref, far_ref, phiq_ref, phik_ref, phik2_ref, prior_ref, dn_ref,
    grad_ref,
):
    member = at_ref[1]
    masks = [
        jnp.concatenate(
            [causal_mask(member, others, late) for others in ((0, 1), (2, 3))], axis=0
        )
        for late in (False, True)
    ]
    pieces = ((own_ref, core_ref), (x_ref, far_ref))

    def both(block, columns):
        return jnp.concatenate([block_rows(refs, block, columns) for refs in pieces], axis=0)

    grad_q = jnp.zeros((FD, HD), F32)
    grad_k = jnp.zeros((FD, HD), F32)
    later = jnp.zeros((PHI, HD), F32)
    later_den = jnp.zeros((PHI, 1), F32)
    for block in reversed(range(BLOCKS)):
        values = both(block, VALUE)
        keys = both(block, KEY)
        queries = block_rows((own_ref,), block, QUERY)
        phi_q = phiq_ref[block]
        phi_q16 = phi_q.astype(BF16)
        phi_k = jnp.concatenate([phik_ref[block], phik2_ref[block]], axis=1)
        grads = dn_ref[block]
        high = grads[:HD]
        d_den = (
            grads[2 * HD:2 * HD + 1].astype(F32) + grads[2 * HD + 1:2 * HD + 2].astype(F32)
        )
        pair = dot(values, high) + d_den
        pair = jnp.where(masks[block // 2], pair, 0.0).astype(BF16)
        phi_k_high, phi_k_low = split(phi_k)
        grad_phi = dot(phi_k_high, pair) + dot(phi_k_low, pair)
        if block > 0:
            prior = prior_ref[block].T
            top, low = split(prior[:, :HD])
            grad_phi = grad_phi + dot(
                jnp.concatenate([top, low], axis=1), jnp.concatenate([high, high], axis=0)
            )
            grad_phi = grad_phi + dot(top, grads[HD:2 * HD])
            grad_phi = grad_phi + prior[:, HD:HD + 1] * d_den
        projected = jnp.concatenate(split(features_back(phi_q, grad_phi)), axis=0)
        product = dot(projected, queries)
        grad_q = grad_q + product[:FD] + product[FD:]

        grad_phi = dot(phi_q16, pair, NT)
        if block < BLOCKS - 1:
            parts = jnp.concatenate(split(later), axis=1)
            doubled = jnp.concatenate([values, values], axis=1)
            grad_phi = grad_phi + dot(parts, doubled, NT) + later_den
        projected = jnp.concatenate(
            split(features_back(phi_k, grad_phi)), axis=0
        )
        product = dot(projected, keys)
        grad_k = grad_k + product[:FD] + product[FD:]
        if block > 0:
            terms = dot(phi_q16, grads, NT)
            later = later + terms[:, :HD] + terms[:, HD:2 * HD]
            later_den = later_den + terms[:, 2 * HD:2 * HD + 1] + terms[:, 2 * HD + 1:2 * HD + 2]
    grad_ref[0] = grad_q.astype(grad_ref.dtype)
    grad_ref[1] = grad_k.astype(grad_ref.dtype)


VMEM = pl.BlockSpec(memory_space=pltpu.VMEM)
SMEM = pl.BlockSpec(memory_space=pltpu.SMEM)
PARAMS = pltpu.CompilerParams(vmem_limit_bytes=40 * 1024 * 1024)
PARTIAL = [
    ((BLOCKS, 1, ROWS), F32),
    ((BLOCKS, 1, ROWS), F32),
    ((BLOCKS, HD, ROWS), F32),
    ((BLOCKS, AUG, ROWS), F32),
    ((BLOCKS, AUG, PHI), F32),
]
PHI_KEYS = ((BLOCKS, PHI, HALF), F32)


def call(kernel, name, outs, args, scratch=(), flops=0):
    return pl.pallas_call(
        kernel,
        out_shape=[jax.ShapeDtypeStruct(*out) for out in outs],
        in_specs=[SMEM] + [VMEM] * (len(args) - 1),
        out_specs=[VMEM] * len(outs),
        scratch_shapes=[pltpu.VMEM(*s) for s in scratch],
        compiler_params=PARAMS,
        cost_estimate=pl.CostEstimate(flops=flops, bytes_accessed=0, transcendentals=0),
        name=name,
    )(*args)


def on_device(queries, keys, values, segment_ids, feat_query, feat_key):
    spot = lax.axis_index("ctx")
    place, member = spot // MEMBERS, spot % MEMBERS
    z_groups = [[j + MEMBERS * k for k in range(PLACES)] for j in range(MEMBERS)]

    def swap(array, relative):
        return lax.ppermute(array, "ctx", [(i, i ^ relative) for i in range(32)])

    def along_z(array):
        return lax.all_to_all(array, "ctx", 0, 0, axis_index_groups=z_groups)

    swapped = segment_ids[0] > segment_ids[1]
    at = jnp.stack([place, member]).astype(jnp.int32)

    (sent,) = call(
        pack_kernel, "pack",
        [((PLACES, 2, SEG, 3 * HD), BF16)],
        (
            segment_ids,
            queries.reshape(2 * SEG * PLACES, HD),
            keys.reshape(2 * SEG, HD),
            values.reshape(2 * SEG, HD),
        ),
        [((2 * SEG * PLACES, HD), F32)],
    )
    own = along_z(sent)
    mine = own[..., :2 * HD]
    beside = swap(mine, 2)
    core = swap(mine, 1)
    far = swap(beside, 1)

    wq = jnp.transpose(feat_query, (0, 2, 1))
    wk = jnp.transpose(feat_key, (0, 2, 1))

    phi_q, *first = call(
        first_kernel, "first_half",
        [((BLOCKS, PHI, ROWS), F32)] + PARTIAL + [PHI_KEYS],
        (at, own, core, wq, wk),
        flops=5 * 10 ** 9,
    )
    student, phi_k2, prior, grads = call(
        second_kernel, "second_half",
        [
            ((PLACES, 2, SEG, HD), BF16),
            PHI_KEYS,
            ((BLOCKS, AUG, PHI), F32),
            ((BLOCKS, 2 * HD + 16, ROWS), BF16),
        ],
        (at, own, beside, far, wk, phi_q, *first[:5]),
        PARTIAL,
        flops=5 * 10 ** 9,
    )
    (grad,) = call(
        backward_kernel, "backward",
        [((2, FD, HD), BF16)],
        (at, own, core, beside, far, phi_q, first[5], phi_k2, prior, grads),
        flops=5 * 10 ** 9,
    )

    sum_groups = [
        [32 * d + MEMBERS * k + j for d in range(2) for j in range(MEMBERS)]
        for k in range(PLACES)
    ]
    shares = lax.all_to_all(
        jnp.broadcast_to(grad, (8,) + grad.shape), ("dp", "ctx"), 0, 0,
        axis_index_groups=sum_groups,
    )
    share = jnp.sum(shares.astype(F32), axis=0).astype(BF16)
    share = jnp.broadcast_to(share, (PLACES,) + share.shape)
    whole = along_z(jnp.concatenate([student, share], axis=-1))
    student = whole[..., :HD]
    student = jnp.where(swapped, student[:, ::-1], student)
    student = jnp.transpose(student, (1, 2, 0, 3)).reshape(2 * SEG, 1, PLACES, HD)
    grads = jnp.transpose(whole[..., HD:], (1, 0, 3, 2)).astype(F32)
    return student, grads[0], grads[1]


def solution(mesh):
    placed = (
        P("ctx", "dp", "tensor", None),
        P("ctx", "dp", "tensor", None),
        P("ctx", "dp", "tensor", None),
        P("ctx"),
        P("tensor", None, None),
        P("tensor", None, None),
    )
    return jax.shard_map(
        on_device,
        mesh=mesh,
        in_specs=placed,
        out_specs=(
            P("ctx", "dp", "tensor", None),
            P("tensor", None, None),
            P("tensor", None, None),
        ),
        check_vma=False,
    )
```

```python
import math

import jax
import jax.numpy as jnp
from jax import lax
from jax.experimental import pallas as pl
from jax.experimental.pallas import tpu as pltpu
from jax.sharding import PartitionSpec as P

PLACES = 8
MEMBERS = 4
SEG = 64
HD = 128
FD = 64
PHI = 2 * FD
BLOCKS = 4
ROWS = 4 * SEG
HALF = 8 * SEG
AUG = HD + 16
LOSS = 1.0 / 8192.0
F32 = jnp.float32
BF16 = jnp.bfloat16
NN = (((1,), (0,)), ((), ()))
NT = (((1,), (1,)), ((), ()))


def dot(a, b, dims=NN):
    return lax.dot_general(a, b, dims, preferred_element_type=F32)


def split(array):
    high = array.astype(BF16)
    return high, (array - high.astype(F32)).astype(BF16)


def causal_mask(member, others, late):
    def turn(who):
        return 3 - who if late else who

    key = lax.broadcasted_iota(jnp.int32, (HALF, 1), 0)
    row = lax.broadcasted_iota(jnp.int32, (1, ROWS), 1)
    second = (key // SEG) % 2
    who = jnp.where(second == 0, member ^ others[0], member ^ others[1])
    key_at = (key // (2 * SEG)) * (4 * SEG) + turn(who) * SEG + key % SEG
    row_at = (row // SEG) * (4 * SEG) + turn(member) * SEG + row % SEG
    return key_at <= row_at


def features(projected):
    top = jnp.max(projected, axis=0, keepdims=True)
    bottom = jnp.min(projected, axis=0, keepdims=True)
    plus = jnp.exp(projected - top)
    minus = jnp.exp(bottom - projected)
    plus = plus * (1.0 / jnp.sum(plus, axis=0, keepdims=True))
    minus = minus * (1.0 / jnp.sum(minus, axis=0, keepdims=True))
    return jnp.concatenate([plus, minus], axis=0)


def features_back(phi, grad):
    term = phi * grad
    plus, minus = term[:FD], term[FD:]
    plus = plus - phi[:FD] * jnp.sum(plus, axis=0, keepdims=True)
    minus = minus - phi[FD:] * jnp.sum(minus, axis=0, keepdims=True)
    return plus - minus


def where_is(chunk):
    return (chunk, 0) if chunk < PLACES else (2 * PLACES - 1 - chunk, 1)


def block_rows(refs, block, columns):
    rows = []
    for chunk in range(4 * block, 4 * block + 4):
        place, late = where_is(chunk)
        rows += [ref[place, late, :, columns] for ref in refs]
    return jnp.concatenate(rows, axis=0)


KEY = slice(0, HD)
VALUE = slice(HD, 2 * HD)
QUERY = slice(0, HD)


def pack_kernel(ids_ref, q_ref, k_ref, v_ref, out_ref, outq_ref, flag_ref, ids, q16, wide, k16, v16, sems):
    copies = [
        pltpu.make_async_copy(source, target, sems.at[i])
        for i, (source, target) in enumerate(
            ((ids_ref, ids), (k_ref, k16), (v_ref, v16), (q_ref, q16))
        )
    ]
    for copy in copies:
        copy.start()
    for copy in copies[:3]:
        copy.wait()
    swapped = ids[0] > ids[1]
    flag_ref[0] = jnp.where(swapped, 1, 0)

    def half_rows(late):
        start = jnp.where(swapped, SEG - SEG * late, SEG * late)
        return pl.multiple_of(start, SEG)

    for late in range(2):
        rows = pl.ds(half_rows(late), SEG)
        pair = jnp.concatenate([k16[rows], v16[rows]], axis=1)
        for place in range(PLACES):
            out_ref[place, late] = pair
    copies[3].wait()
    wide[...] = q16[...].astype(F32)
    for late in range(2):
        for place in range(PLACES):
            rows = pl.ds(half_rows(late) * PLACES + place, SEG, stride=PLACES)
            outq_ref[place, late] = wide[rows].astype(BF16)


def tie_kernel(value_ref, token_ref, out_ref):
    pass


def pair_kernel(one_ref, two_ref, out_ref):
    out_ref[...] = (one_ref[...] + two_ref[...]).astype(BF16)


def share_kernel(a_ref, b_ref, c_ref, d_ref, student_ref, out_ref):
    one = a_ref[...].astype(F32) + b_ref[...].astype(F32)
    two = c_ref[...].astype(F32) + d_ref[...].astype(F32)
    total = (one + two).astype(BF16)
    for place in range(PLACES):
        out_ref[place, :, :, :HD] = student_ref[place]
        out_ref[place, :, :, HD:] = total


def finish_kernel(flag_ref, whole_ref, student_ref, gq_ref, gk_ref, wide):
    for place in range(PLACES):
        gq_ref[place] = whole_ref[place, 0, :, HD:].astype(F32)
        gk_ref[place] = whole_ref[place, 1, :, HD:].astype(F32)
    swapped = flag_ref[0] == 1
    for late in range(2):
        start = pl.multiple_of(jnp.where(swapped, SEG - SEG * late, SEG * late), SEG)
        for place in range(PLACES):
            rows = pl.ds(start * PLACES + place, SEG, stride=PLACES)
            wide[rows] = whole_ref[place, late, :, :HD].astype(F32)
    student_ref[...] = wide[...].astype(BF16)


def half_forward(refs, masks, queries, phi_q, wk, outs):
    top_ref, total_ref, acc_ref, num_ref, state_ref, phik_ref = outs
    scale = (HD ** -0.5) * math.log2(math.e)
    keys, values_t = [], []
    for block in range(BLOCKS):
        keys.append(block_rows(refs, block, KEY))
        value = block_rows(refs, block, VALUE).T
        values_t.append(jnp.concatenate([value, jnp.ones((AUG - HD, HALF), BF16)], axis=0))
    for block in range(BLOCKS):
        phi = features(dot(wk, keys[block], NT))
        phik_ref[block] = phi
        phi16 = phi.astype(BF16)
        state_ref[block] = dot(values_t[block], phi16, NT)
        pair = dot(phi16.T, phi_q[block])
        pair = jnp.where(masks[block // 2], pair, 0.0)
        if block == 0:
            high, low = split(pair)
            num_ref[block] = dot(values_t[block], high) + dot(values_t[block], low)
        else:
            num_ref[block] = dot(values_t[block], pair.astype(BF16))

        scores = [dot(keys[b], queries[block], NT) for b in range(block + 1)]
        scores[-1] = jnp.where(masks[block // 2], scores[-1], -1e30)
        top = jnp.max(scores[0], axis=0, keepdims=True)
        for s in scores[1:]:
            top = jnp.maximum(top, jnp.max(s, axis=0, keepdims=True))
        total, acc = 0.0, 0.0
        for b, s in enumerate(scores):
            weights = jnp.exp2(s * scale - top * scale)
            total = total + jnp.sum(weights, axis=0, keepdims=True)
            acc = acc + dot(values_t[b][:HD], weights.astype(BF16))
        top_ref[block] = top * scale
        total_ref[block] = total
        acc_ref[block] = acc


def first_kernel(at_ref, rows_ref, own_ref, core_ref, wq_ref, wk_ref, phiq_ref, *outs):
    place, member = at_ref[0], at_ref[1]
    masks = [causal_mask(member, (0, 1), late) for late in (False, True)]
    queries = [block_rows((rows_ref,), b, QUERY) for b in range(BLOCKS)]
    phi_q = []
    for block in range(BLOCKS):
        phi = features(dot(wq_ref[place], queries[block], NT))
        phiq_ref[block] = phi
        phi_q.append(phi.astype(BF16))
    half_forward((own_ref, core_ref), masks, queries, phi_q, wk_ref[place], outs)


def second_kernel(
    at_ref, rows_ref, x_ref, far_ref, wk_ref, phiq_ref,
    top_ref, total_ref, acc_ref, num_ref, state_ref,
    student_ref, phik_ref, prior_ref, dn_ref,
    top2_ref, total2_ref, acc2_ref, num2_ref, state2_ref,
):
    place, member = at_ref[0], at_ref[1]
    masks = [causal_mask(member, (2, 3), late) for late in (False, True)]
    queries = [block_rows((rows_ref,), b, QUERY) for b in range(BLOCKS)]
    phi_q = [phiq_ref[block].astype(BF16) for block in range(BLOCKS)]
    outs = (top2_ref, total2_ref, acc2_ref, num2_ref, state2_ref, phik_ref)
    half_forward((x_ref, far_ref), masks, queries, phi_q, wk_ref[place], outs)
    prior = jnp.zeros((AUG, PHI), F32)
    for block in range(BLOCKS):
        top = jnp.maximum(top_ref[block], top2_ref[block])
        one = jnp.exp2(top_ref[block] - top)
        two = jnp.exp2(top2_ref[block] - top)
        total = total_ref[block] * one + total2_ref[block] * two
        teacher = (acc_ref[block] * one + acc2_ref[block] * two) * (1.0 / total)
        prior_ref[block] = prior
        numerator = num_ref[block] + num2_ref[block]
        if block > 0:
            numerator = numerator + dot(prior.astype(BF16), phi_q[block])
        prior = prior + state_ref[block] + state2_ref[block]
        inverse = 1.0 / numerator[HD:HD + 1]
        y = numerator[:HD] * inverse
        d_num = (y - teacher) * (inverse * LOSS)
        d_den = -jnp.sum(d_num * y, axis=0, keepdims=True)
        den_high, den_low = split(d_den)
        index = lax.broadcasted_iota(jnp.int32, (AUG - HD, ROWS), 0)
        extra = jnp.where(
            index == 0, den_high.astype(F32), jnp.where(index == 1, den_low.astype(F32), 0.0)
        )
        dn_ref[block] = jnp.concatenate([d_num.astype(BF16), extra.astype(BF16)], axis=0)
        rows = y.T.astype(BF16)
        for i in range(4):
            place, late = where_is(4 * block + i)
            student_ref[place, late] = rows[i * SEG:(i + 1) * SEG]


def backward_kernel(
    at_ref, rows_ref, own_ref, core_ref, x_ref, far_ref, phiq_ref, phik_ref, phik2_ref, prior_ref, dn_ref,
    grad_ref,
):
    member = at_ref[1]
    masks = [
        jnp.concatenate(
            [causal_mask(member, others, late) for others in ((0, 1), (2, 3))], axis=0
        )
        for late in (False, True)
    ]
    pieces = ((own_ref, core_ref), (x_ref, far_ref))

    def both(block, columns):
        return jnp.concatenate([block_rows(refs, block, columns) for refs in pieces], axis=0)

    def project(phi, grad, rows, exact):
        back = features_back(phi, grad)
        if not exact:
            return dot(back.astype(BF16), rows)
        product = dot(jnp.concatenate(split(back), axis=0), rows)
        return product[:FD] + product[FD:]

    grad_q = jnp.zeros((FD, HD), F32)
    grad_k = jnp.zeros((FD, HD), F32)
    later = jnp.zeros((PHI, AUG), F32)
    for block in reversed(range(BLOCKS)):
        first = block == 0
        values = both(block, VALUE)
        keys = both(block, KEY)
        queries = block_rows((rows_ref,), block, QUERY)
        phi_q = phiq_ref[block]
        phi_q16 = phi_q.astype(BF16)
        phi_k = jnp.concatenate([phik_ref[block], phik2_ref[block]], axis=1)
        grads = dn_ref[block]
        d_den = grads[HD:HD + 1].astype(F32) + grads[HD + 1:HD + 2].astype(F32)
        pair = dot(values, grads[:HD]) + d_den
        pair = jnp.where(masks[block // 2], pair, 0.0).astype(BF16)
        if first:
            grad_phi = dot(jnp.concatenate(split(phi_k), axis=0), pair)
            grad_phi = grad_phi[:PHI] + grad_phi[PHI:]
        else:
            prior = prior_ref[block].T
            grad_phi = dot(phi_k.astype(BF16), pair) + dot(prior.astype(BF16), grads)
        grad_q = grad_q + project(phi_q, grad_phi, queries, first)

        if block == BLOCKS - 1:
            grad_phi = dot(phi_q16, pair, NT)
        else:
            grad_phi = dot(
                jnp.concatenate([phi_q16, later[:, :HD].astype(BF16)], axis=1),
                jnp.concatenate([pair, values], axis=1),
                NT,
            )
            grad_phi = grad_phi + (later[:, HD:HD + 1] + later[:, HD + 1:HD + 2])
        grad_k = grad_k + project(phi_k, grad_phi, keys, first)
        if not first:
            later = later + dot(phi_q16, grads, NT)
    grad_ref[0] = grad_q.astype(grad_ref.dtype)
    grad_ref[1] = grad_k.astype(grad_ref.dtype)


VMEM = pl.BlockSpec(memory_space=pltpu.VMEM)
SMEM = pl.BlockSpec(memory_space=pltpu.SMEM)
ANY = pl.BlockSpec(memory_space=pl.ANY)
PARAMS = pltpu.CompilerParams(vmem_limit_bytes=8 * 1024 * 1024)
PARTIAL = [
    ((BLOCKS, 1, ROWS), F32),
    ((BLOCKS, 1, ROWS), F32),
    ((BLOCKS, HD, ROWS), F32),
    ((BLOCKS, AUG, ROWS), F32),
    ((BLOCKS, AUG, PHI), F32),
]
PHI_KEYS = ((BLOCKS, PHI, HALF), F32)


def call(kernel, name, outs, args, scratch=(), flops=0, smem=True):
    return pl.pallas_call(
        kernel,
        out_shape=[jax.ShapeDtypeStruct(*out) for out in outs],
        in_specs=[SMEM if smem else VMEM] + [VMEM] * (len(args) - 1),
        out_specs=[VMEM] * len(outs),
        scratch_shapes=[pltpu.VMEM(*s) for s in scratch],
        compiler_params=PARAMS,
        cost_estimate=pl.CostEstimate(flops=flops, bytes_accessed=0, transcendentals=0),
        name=name,
    )(*args)


def tied(array, token):
    return pl.pallas_call(
        tie_kernel,
        out_shape=jax.ShapeDtypeStruct(array.shape, array.dtype),
        in_specs=[ANY, ANY],
        out_specs=ANY,
        input_output_aliases={0: 0},
        compiler_params=pltpu.CompilerParams(vmem_limit_bytes=1024 * 1024),
        name="tie",
    )(array, token)


def on_device(queries, keys, values, segment_ids, feat_query, feat_key):
    spot = lax.axis_index("ctx")
    place, member = spot // MEMBERS, spot % MEMBERS
    z_groups = [[j + MEMBERS * k for k in range(PLACES)] for j in range(MEMBERS)]

    def swap(array, relative):
        return lax.ppermute(array, "ctx", [(i, i ^ relative) for i in range(32)])

    def along_z(array):
        return lax.all_to_all(array, "ctx", 0, 0, axis_index_groups=z_groups)

    at = jnp.stack([place, member]).astype(jnp.int32)

    sent, sent_q, flag = pl.pallas_call(
        pack_kernel,
        out_shape=[
            jax.ShapeDtypeStruct((PLACES, 2, SEG, 2 * HD), BF16),
            jax.ShapeDtypeStruct((PLACES, 2, SEG, HD), BF16),
            jax.ShapeDtypeStruct((1,), jnp.int32),
        ],
        in_specs=[ANY] * 4,
        out_specs=[VMEM, VMEM, SMEM],
        scratch_shapes=[
            pltpu.SMEM((2,), jnp.int32),
            pltpu.VMEM((2 * SEG * PLACES, HD), BF16),
            pltpu.VMEM((2 * SEG * PLACES, HD), F32),
            pltpu.VMEM((2 * SEG, HD), BF16),
            pltpu.VMEM((2 * SEG, HD), BF16),
            pltpu.SemaphoreType.DMA((4,)),
        ],
        compiler_params=pltpu.CompilerParams(vmem_limit_bytes=62 * 1024 * 1024),
        name="pack",
    )(
        segment_ids,
        queries.reshape(2 * SEG * PLACES, HD),
        keys.reshape(2 * SEG, HD),
        values.reshape(2 * SEG, HD),
    )
    own = along_z(sent)
    beside = swap(own, 2)
    core = swap(own, 1)
    rows = along_z(tied(sent_q, own))

    wq = jnp.transpose(feat_query, (0, 2, 1))
    wk = jnp.transpose(feat_key, (0, 2, 1))

    phi_q, *first = call(
        first_kernel, "first_half",
        [((BLOCKS, PHI, ROWS), F32)] + PARTIAL + [PHI_KEYS],
        (at, rows, own, core, wq, wk),
        flops=5 * 10 ** 9,
    )
    beside = tied(beside, rows)
    far = swap(beside, 1)
    student, phi_k2, prior, grads = call(
        second_kernel, "second_half",
        [
            ((PLACES, 2, SEG, HD), BF16),
            PHI_KEYS,
            ((BLOCKS, AUG, PHI), F32),
            ((BLOCKS, AUG, ROWS), BF16),
        ],
        (at, rows, beside, far, wk, phi_q, *first[:5]),
        PARTIAL,
        flops=5 * 10 ** 9,
    )
    (grad,) = call(
        backward_kernel, "backward",
        [((2, FD, HD), F32)],
        (at, rows, own, core, beside, far, phi_q, first[5], phi_k2, prior, grads),
        flops=5 * 10 ** 9,
    )

    def swap_wide(array, relative):
        pairs = [(i, i ^ relative) for i in range(64)]
        return lax.ppermute(array, ("dp", "ctx"), pairs)

    (pair,) = call(
        pair_kernel, "pair", [((2, FD, HD), BF16)], (grad, swap(grad, 1)), smem=False
    )
    (share,) = call(
        share_kernel, "share", [((PLACES, 2, SEG, 2 * HD), BF16)],
        (pair, swap_wide(pair, 2), swap_wide(pair, 32), swap_wide(pair, 34), student),
        smem=False,
    )
    whole = along_z(share)
    student, grad_query, grad_key = pl.pallas_call(
        finish_kernel,
        out_shape=[
            jax.ShapeDtypeStruct((2 * SEG * PLACES, HD), BF16),
            jax.ShapeDtypeStruct((PLACES, FD, HD), F32),
            jax.ShapeDtypeStruct((PLACES, FD, HD), F32),
        ],
        in_specs=[SMEM, VMEM],
        out_specs=[VMEM] * 3,
        scratch_shapes=[pltpu.VMEM((2 * SEG * PLACES, HD), F32)],
        compiler_params=PARAMS,
        name="finish",
    )(flag, whole)
    student = student.reshape(2 * SEG, 1, PLACES, HD)
    return student, jnp.transpose(grad_query, (0, 2, 1)), jnp.transpose(grad_key, (0, 2, 1))


def solution(mesh):
    placed = (
        P("ctx", "dp", "tensor", None),
        P("ctx", "dp", "tensor", None),
        P("ctx", "dp", "tensor", None),
        P("ctx"),
        P("tensor", None, None),
        P("tensor", None, None),
    )
    return jax.shard_map(
        on_device,
        mesh=mesh,
        in_specs=placed,
        out_specs=(
            P("ctx", "dp", "tensor", None),
            P("tensor", None, None),
            P("tensor", None, None),
        ),
        check_vma=False,
    )
```

```python
import math

import jax
import jax.numpy as jnp
from jax import lax
from jax.experimental import pallas as pl
from jax.experimental.pallas import tpu as pltpu
from jax.sharding import PartitionSpec as P

PLACES = 8
MEMBERS = 4
SEG = 64
HD = 128
FD = 64
PHI = 2 * FD
BLOCKS = 4
ROWS = 4 * SEG
HALF = 8 * SEG
AUG = HD + 16
LOSS = 1.0 / 8192.0
F32 = jnp.float32
BF16 = jnp.bfloat16
NN = (((1,), (0,)), ((), ()))
NT = (((1,), (1,)), ((), ()))


def dot(a, b, dims=NN):
    return lax.dot_general(a, b, dims, preferred_element_type=F32)


def split(array):
    high = array.astype(BF16)
    return high, (array - high.astype(F32)).astype(BF16)


def causal_mask(member, others, late):
    def turn(who):
        return 3 - who if late else who

    key = lax.broadcasted_iota(jnp.int32, (HALF, 1), 0)
    row = lax.broadcasted_iota(jnp.int32, (1, ROWS), 1)
    second = (key // SEG) % 2
    who = jnp.where(second == 0, member ^ others[0], member ^ others[1])
    key_at = (key // (2 * SEG)) * (4 * SEG) + turn(who) * SEG + key % SEG
    row_at = (row // SEG) * (4 * SEG) + turn(member) * SEG + row % SEG
    return key_at <= row_at


def features(projected):
    top = jnp.max(projected, axis=0, keepdims=True)
    bottom = jnp.min(projected, axis=0, keepdims=True)
    plus = jnp.exp(projected - top)
    minus = jnp.exp(bottom - projected)
    plus = plus * (1.0 / jnp.sum(plus, axis=0, keepdims=True))
    minus = minus * (1.0 / jnp.sum(minus, axis=0, keepdims=True))
    return jnp.concatenate([plus, minus], axis=0)


def features_back(phi, grad):
    term = phi * grad
    plus, minus = term[:FD], term[FD:]
    plus = plus - phi[:FD] * jnp.sum(plus, axis=0, keepdims=True)
    minus = minus - phi[FD:] * jnp.sum(minus, axis=0, keepdims=True)
    return plus - minus


def where_is(chunk):
    return (chunk, 0) if chunk < PLACES else (2 * PLACES - 1 - chunk, 1)


def block_rows(refs, block, columns):
    rows = []
    for chunk in range(4 * block, 4 * block + 4):
        place, late = where_is(chunk)
        rows += [ref[place, late, :, columns] for ref in refs]
    return jnp.concatenate(rows, axis=0)


KEY = slice(0, HD)
VALUE = slice(HD, 2 * HD)
QUERY = slice(0, HD)


def pack_kernel(ids_ref, q_ref, k_ref, v_ref, out_ref, outq_ref, flag_ref, ids, q16, wide, k16, v16, sems):
    copies = [
        pltpu.make_async_copy(source, target, sems.at[i])
        for i, (source, target) in enumerate(
            ((ids_ref, ids), (k_ref, k16), (v_ref, v16), (q_ref, q16))
        )
    ]
    for copy in copies:
        copy.start()
    for copy in copies[:3]:
        copy.wait()
    swapped = ids[0] > ids[1]
    flag_ref[0] = jnp.where(swapped, 1, 0)

    def half_rows(late):
        start = jnp.where(swapped, SEG - SEG * late, SEG * late)
        return pl.multiple_of(start, SEG)

    for late in range(2):
        rows = pl.ds(half_rows(late), SEG)
        pair = jnp.concatenate([k16[rows], v16[rows]], axis=1)
        for place in range(PLACES):
            out_ref[place, late] = pair
    copies[3].wait()
    wide[...] = q16[...].astype(F32)
    for late in range(2):
        for place in range(PLACES):
            rows = pl.ds(half_rows(late) * PLACES + place, SEG, stride=PLACES)
            outq_ref[place, late] = wide[rows].astype(BF16)


def tie_kernel(value_ref, token_ref, out_ref):
    pass


def pair_kernel(one_ref, two_ref, out_ref):
    out_ref[...] = (one_ref[...] + two_ref[...]).astype(BF16)


def share_kernel(a_ref, b_ref, c_ref, d_ref, student_ref, out_ref):
    one = a_ref[...].astype(F32) + b_ref[...].astype(F32)
    two = c_ref[...].astype(F32) + d_ref[...].astype(F32)
    total = (one + two).astype(BF16)
    for place in range(PLACES):
        out_ref[place, :, :, :HD] = student_ref[place]
        out_ref[place, :, :, HD:] = total


def finish_kernel(flag_ref, whole_ref, student_ref, gq_ref, gk_ref, wide):
    for place in range(PLACES):
        gq_ref[place] = whole_ref[place, 0, :, HD:].astype(F32)
        gk_ref[place] = whole_ref[place, 1, :, HD:].astype(F32)
    swapped = flag_ref[0] == 1
    for late in range(2):
        start = pl.multiple_of(jnp.where(swapped, SEG - SEG * late, SEG * late), SEG)
        for place in range(PLACES):
            rows = pl.ds(start * PLACES + place, SEG, stride=PLACES)
            wide[rows] = whole_ref[place, late, :, :HD].astype(F32)
    student_ref[...] = wide[...].astype(BF16)


def half_forward(refs, masks, queries, phi_q, wk, outs):
    top_ref, total_ref, acc_ref, num_ref, state_ref, phik_ref = outs
    scale = (HD ** -0.5) * math.log2(math.e)
    keys, values_t = [], []
    for block in range(BLOCKS):
        keys.append(block_rows(refs, block, KEY))
        value = block_rows(refs, block, VALUE).T
        values_t.append(jnp.concatenate([value, jnp.ones((AUG - HD, HALF), BF16)], axis=0))
    def scores_of(block):
        scores = [dot(keys[b], queries[block], NT) for b in range(block + 1)]
        scores[-1] = jnp.where(masks[block // 2], scores[-1], -1e30)
        top = jnp.max(scores[0], axis=0, keepdims=True)
        for s in scores[1:]:
            top = jnp.maximum(top, jnp.max(s, axis=0, keepdims=True))
        return scores, top

    ready = [scores_of(block) for block in range(BLOCKS)]
    for block in range(BLOCKS):
        scores, top = ready[block]
        total, acc = 0.0, 0.0
        for b, s in enumerate(scores):
            weights = jnp.exp2(s * scale - top * scale)
            total = total + jnp.sum(weights, axis=0, keepdims=True)
            acc = acc + dot(values_t[b][:HD], weights.astype(BF16))
        top_ref[block] = top * scale
        total_ref[block] = total
        acc_ref[block] = acc
    phis = [features(dot(wk, keys[b], NT)) for b in range(BLOCKS)]
    phi16s = [phi.astype(BF16) for phi in phis]
    pairs = [dot(phi16s[b], phi_q[b], (((0,), (0,)), ((), ()))) for b in range(BLOCKS)]
    for b in range(BLOCKS):
        phik_ref[b] = phis[b]
        state_ref[b] = dot(values_t[b], phi16s[b], NT)
    pairs = [jnp.where(masks[b // 2], pairs[b], 0.0) for b in range(BLOCKS)]
    high, low = split(pairs[0])
    num_ref[0] = dot(values_t[0], high) + dot(values_t[0], low)
    for b in range(1, BLOCKS):
        num_ref[b] = dot(values_t[b], pairs[b].astype(BF16))


def first_kernel(at_ref, rows_ref, own_ref, core_ref, wq_ref, wk_ref, phiq_ref, *outs):
    place, member = at_ref[0], at_ref[1]
    masks = [causal_mask(member, (0, 1), late) for late in (False, True)]
    queries = [block_rows((rows_ref,), b, QUERY) for b in range(BLOCKS)]
    phi_q = []
    for block in range(BLOCKS):
        phi = features(dot(wq_ref[place], queries[block], NT))
        phiq_ref[block] = phi
        phi_q.append(phi.astype(BF16))
    half_forward((own_ref, core_ref), masks, queries, phi_q, wk_ref[place], outs)


def second_kernel(
    at_ref, rows_ref, x_ref, far_ref, wk_ref, phiq_ref,
    top_ref, total_ref, acc_ref, num_ref, state_ref,
    student_ref, phik_ref, prior_ref, dn_ref,
    top2_ref, total2_ref, acc2_ref, num2_ref, state2_ref,
):
    place, member = at_ref[0], at_ref[1]
    masks = [causal_mask(member, (2, 3), late) for late in (False, True)]
    queries = [block_rows((rows_ref,), b, QUERY) for b in range(BLOCKS)]
    phi_q = [phiq_ref[block].astype(BF16) for block in range(BLOCKS)]
    outs = (top2_ref, total2_ref, acc2_ref, num2_ref, state2_ref, phik_ref)
    half_forward((x_ref, far_ref), masks, queries, phi_q, wk_ref[place], outs)
    span = range(BLOCKS)
    priors = [None] * BLOCKS
    prior = state_ref[0] + state2_ref[0]
    prior_ref[0] = jnp.zeros((AUG, PHI), F32)
    for b in range(1, BLOCKS):
        priors[b] = prior
        prior_ref[b] = prior
        prior = prior + state_ref[b] + state2_ref[b]
    numerators = [num_ref[b] + num2_ref[b] for b in span]
    for b in range(1, BLOCKS):
        numerators[b] = numerators[b] + dot(priors[b].astype(BF16), phi_q[b])
    teachers = []
    for b in span:
        top = jnp.maximum(top_ref[b], top2_ref[b])
        one = jnp.exp2(top_ref[b] - top)
        two = jnp.exp2(top2_ref[b] - top)
        total = total_ref[b] * one + total2_ref[b] * two
        teachers.append((acc_ref[b] * one + acc2_ref[b] * two) * (1.0 / total))
    inverses = [1.0 / numerators[b][HD:HD + 1] for b in span]
    ys = [numerators[b][:HD] * inverses[b] for b in span]
    index = lax.broadcasted_iota(jnp.int32, (AUG - HD, ROWS), 0)
    for b in span:
        d_num = (ys[b] - teachers[b]) * (inverses[b] * LOSS)
        d_den = -jnp.sum(d_num * ys[b], axis=0, keepdims=True)
        den_high, den_low = split(d_den)
        extra = jnp.where(
            index == 0, den_high.astype(F32), jnp.where(index == 1, den_low.astype(F32), 0.0)
        )
        dn_ref[b] = jnp.concatenate([d_num.astype(BF16), extra.astype(BF16)], axis=0)
    for b in span:
        rows = ys[b].astype(BF16).T
        for i in range(4):
            place, late = where_is(4 * b + i)
            student_ref[place, late] = rows[i * SEG:(i + 1) * SEG]


def backward_kernel(
    at_ref, rows_ref, own_ref, core_ref, x_ref, far_ref, phiq_ref, phik_ref, phik2_ref, prior_ref, dn_ref,
    grad_ref,
):
    member = at_ref[1]
    masks = [
        jnp.concatenate(
            [causal_mask(member, others, late) for others in ((0, 1), (2, 3))], axis=0
        )
        for late in (False, True)
    ]
    pieces = ((own_ref, core_ref), (x_ref, far_ref))

    def both(block, columns):
        return jnp.concatenate([block_rows(refs, block, columns) for refs in pieces], axis=0)

    def project(phi, grad, rows, exact):
        back = features_back(phi, grad)
        if not exact:
            return dot(back.astype(BF16), rows)
        product = dot(jnp.concatenate(split(back), axis=0), rows)
        return product[:FD] + product[FD:]

    span = range(BLOCKS)
    values = [both(b, VALUE) for b in span]
    keys = [both(b, KEY) for b in span]
    queries = [block_rows((rows_ref,), b, QUERY) for b in span]
    phi_q = [phiq_ref[b] for b in span]
    phi_q16 = [p.astype(BF16) for p in phi_q]
    phi_k = [jnp.concatenate([phik_ref[b], phik2_ref[b]], axis=1) for b in span]
    grads = [dn_ref[b] for b in span]
    pairs = []
    for b in span:
        d_den = grads[b][HD:HD + 1].astype(F32) + grads[b][HD + 1:HD + 2].astype(F32)
        pair = dot(values[b], grads[b][:HD]) + d_den
        pairs.append(jnp.where(masks[b // 2], pair, 0.0).astype(BF16))
    terms = [dot(phi_q16[b], grads[b], NT) if b > 0 else None for b in span]
    later = [None] * BLOCKS
    total = terms[3]
    for b in (2, 1, 0):
        later[b] = total
        if b > 0:
            total = total + terms[b]
    grad_phi_q = []
    for b in span:
        if b == 0:
            both_terms = dot(jnp.concatenate(split(phi_k[b]), axis=0), pairs[b])
            grad_phi_q.append(both_terms[:PHI] + both_terms[PHI:])
        else:
            prior = prior_ref[b].T
            grad_phi_q.append(
                dot(phi_k[b].astype(BF16), pairs[b]) + dot(prior.astype(BF16), grads[b])
            )
    grad_phi_k = []
    for b in span:
        if b == BLOCKS - 1:
            grad_phi_k.append(dot(phi_q16[b], pairs[b], NT))
        else:
            grad = dot(
                jnp.concatenate([phi_q16[b], later[b][:, :HD].astype(BF16)], axis=1),
                jnp.concatenate([pairs[b], values[b]], axis=1),
                NT,
            )
            grad_phi_k.append(grad + (later[b][:, HD:HD + 1] + later[b][:, HD + 1:HD + 2]))
    grad_q = project(phi_q[0], grad_phi_q[0], queries[0], True)
    for b in range(1, BLOCKS):
        grad_q = grad_q + project(phi_q[b], grad_phi_q[b], queries[b], False)
    grad_k = project(phi_k[0], grad_phi_k[0], keys[0], True)
    for b in range(1, BLOCKS):
        grad_k = grad_k + project(phi_k[b], grad_phi_k[b], keys[b], False)
    grad_ref[0] = grad_q.astype(grad_ref.dtype)
    grad_ref[1] = grad_k.astype(grad_ref.dtype)


def rest_kernel(
    at_ref, rows_ref, own_ref, core_ref, x_ref, far_ref, wk_ref, phiq_ref,
    top_ref, total_ref, acc_ref, num_ref, state_ref, phik_ref,
    student_ref, grad_ref,
    phik2_ref, prior_ref, dn_ref, *partial,
):
    second_kernel(
        at_ref, rows_ref, x_ref, far_ref, wk_ref, phiq_ref,
        top_ref, total_ref, acc_ref, num_ref, state_ref,
        student_ref, phik2_ref, prior_ref, dn_ref, *partial,
    )
    backward_kernel(
        at_ref, rows_ref, own_ref, core_ref, x_ref, far_ref, phiq_ref, phik_ref, phik2_ref,
        prior_ref, dn_ref, grad_ref,
    )


VMEM = pl.BlockSpec(memory_space=pltpu.VMEM)
SMEM = pl.BlockSpec(memory_space=pltpu.SMEM)
ANY = pl.BlockSpec(memory_space=pl.ANY)
PARAMS = pltpu.CompilerParams(vmem_limit_bytes=8 * 1024 * 1024)
PARTIAL = [
    ((BLOCKS, 1, ROWS), F32),
    ((BLOCKS, 1, ROWS), F32),
    ((BLOCKS, HD, ROWS), F32),
    ((BLOCKS, AUG, ROWS), F32),
    ((BLOCKS, AUG, PHI), F32),
]
PHI_KEYS = ((BLOCKS, PHI, HALF), F32)


def call(kernel, name, outs, args, scratch=(), flops=0, smem=True):
    return pl.pallas_call(
        kernel,
        out_shape=[jax.ShapeDtypeStruct(*out) for out in outs],
        in_specs=[SMEM if smem else VMEM] + [VMEM] * (len(args) - 1),
        out_specs=[VMEM] * len(outs),
        scratch_shapes=[pltpu.VMEM(*s) for s in scratch],
        compiler_params=PARAMS,
        cost_estimate=pl.CostEstimate(flops=flops, bytes_accessed=0, transcendentals=0),
        name=name,
    )(*args)


def tied(array, token):
    return pl.pallas_call(
        tie_kernel,
        out_shape=jax.ShapeDtypeStruct(array.shape, array.dtype),
        in_specs=[ANY, ANY],
        out_specs=ANY,
        input_output_aliases={0: 0},
        compiler_params=pltpu.CompilerParams(vmem_limit_bytes=1024 * 1024),
        name="tie",
    )(array, token)


def on_device(queries, keys, values, segment_ids, feat_query, feat_key):
    spot = lax.axis_index("ctx")
    place, member = spot // MEMBERS, spot % MEMBERS
    z_groups = [[j + MEMBERS * k for k in range(PLACES)] for j in range(MEMBERS)]

    def swap(array, relative):
        return lax.ppermute(array, "ctx", [(i, i ^ relative) for i in range(32)])

    def along_z(array):
        return lax.all_to_all(array, "ctx", 0, 0, axis_index_groups=z_groups)

    at = jnp.stack([place, member]).astype(jnp.int32)

    sent, sent_q, flag = pl.pallas_call(
        pack_kernel,
        out_shape=[
            jax.ShapeDtypeStruct((PLACES, 2, SEG, 2 * HD), BF16),
            jax.ShapeDtypeStruct((PLACES, 2, SEG, HD), BF16),
            jax.ShapeDtypeStruct((1,), jnp.int32),
        ],
        in_specs=[ANY] * 4,
        out_specs=[VMEM, VMEM, SMEM],
        scratch_shapes=[
            pltpu.SMEM((2,), jnp.int32),
            pltpu.VMEM((2 * SEG * PLACES, HD), BF16),
            pltpu.VMEM((2 * SEG * PLACES, HD), F32),
            pltpu.VMEM((2 * SEG, HD), BF16),
            pltpu.VMEM((2 * SEG, HD), BF16),
            pltpu.SemaphoreType.DMA((4,)),
        ],
        compiler_params=pltpu.CompilerParams(vmem_limit_bytes=62 * 1024 * 1024),
        name="pack",
    )(
        segment_ids,
        queries.reshape(2 * SEG * PLACES, HD),
        keys.reshape(2 * SEG, HD),
        values.reshape(2 * SEG, HD),
    )
    own = along_z(sent)
    beside = swap(own, 2)
    core = swap(own, 1)
    rows = along_z(tied(sent_q, own))

    wq = jnp.transpose(feat_query, (0, 2, 1))
    wk = jnp.transpose(feat_key, (0, 2, 1))

    phi_q, *first = call(
        first_kernel, "first_half",
        [((BLOCKS, PHI, ROWS), F32)] + PARTIAL + [PHI_KEYS],
        (at, rows, own, core, wq, wk),
        flops=5 * 10 ** 9,
    )
    beside = tied(beside, rows)
    far = swap(beside, 1)
    student, grad = call(
        rest_kernel, "rest",
        [((PLACES, 2, SEG, HD), BF16), ((2, FD, HD), F32)],
        (at, rows, own, core, beside, far, wk, phi_q, *first),
        [PHI_KEYS, ((BLOCKS, AUG, PHI), F32), ((BLOCKS, AUG, ROWS), BF16)] + PARTIAL,
        flops=10 ** 10,
    )
    def swap_wide(array, relative):
        pairs = [(i, i ^ relative) for i in range(64)]
        return lax.ppermute(array, ("dp", "ctx"), pairs)

    (pair,) = call(
        pair_kernel, "pair", [((2, FD, HD), BF16)], (grad, swap(grad, 1)), smem=False
    )
    (share,) = call(
        share_kernel, "share", [((PLACES, 2, SEG, 2 * HD), BF16)],
        (pair, swap_wide(pair, 2), swap_wide(pair, 32), swap_wide(pair, 34), student),
        smem=False,
    )
    whole = along_z(share)
    student, grad_query, grad_key = pl.pallas_call(
        finish_kernel,
        out_shape=[
            jax.ShapeDtypeStruct((2 * SEG * PLACES, HD), BF16),
            jax.ShapeDtypeStruct((PLACES, FD, HD), F32),
            jax.ShapeDtypeStruct((PLACES, FD, HD), F32),
        ],
        in_specs=[SMEM, VMEM],
        out_specs=[VMEM] * 3,
        scratch_shapes=[pltpu.VMEM((2 * SEG * PLACES, HD), F32)],
        compiler_params=PARAMS,
        name="finish",
    )(flag, whole)
    student = student.reshape(2 * SEG, 1, PLACES, HD)
    return student, jnp.transpose(grad_query, (0, 2, 1)), jnp.transpose(grad_key, (0, 2, 1))


def solution(mesh):
    placed = (
        P("ctx", "dp", "tensor", None),
        P("ctx", "dp", "tensor", None),
        P("ctx", "dp", "tensor", None),
        P("ctx"),
        P("tensor", None, None),
        P("tensor", None, None),
    )
    return jax.shard_map(
        on_device,
        mesh=mesh,
        in_specs=placed,
        out_specs=(
            P("ctx", "dp", "tensor", None),
            P("tensor", None, None),
            P("tensor", None, None),
        ),
        check_vma=False,
    )
```

```python
import math

import jax
import jax.numpy as jnp
from jax import lax
from jax.experimental import pallas as pl
from jax.experimental.pallas import tpu as pltpu
from jax.sharding import PartitionSpec as P

PLACES = 8
MEMBERS = 4
SEG = 64
HD = 128
FD = 64
PHI = 2 * FD
BLOCKS = 4
ROWS = 4 * SEG
HALF = 8 * SEG
AUG = HD + 16
LOSS = 1.0 / 8192.0
SCALE = (HD ** -0.5) * math.log2(math.e)
F32 = jnp.float32
BF16 = jnp.bfloat16
NN = (((1,), (0,)), ((), ()))
NT = (((1,), (1,)), ((), ()))


def dot(a, b, dims=NN):
    return lax.dot_general(a, b, dims, preferred_element_type=F32)


def split(array):
    high = array.astype(BF16)
    return high, (array - high.astype(F32)).astype(BF16)


def causal_mask(member, others, late):
    def turn(who):
        return 3 - who if late else who

    key = lax.broadcasted_iota(jnp.int32, (HALF, 1), 0)
    row = lax.broadcasted_iota(jnp.int32, (1, ROWS), 1)
    second = (key // SEG) % 2
    who = jnp.where(second == 0, member ^ others[0], member ^ others[1])
    key_at = (key // (2 * SEG)) * (4 * SEG) + turn(who) * SEG + key % SEG
    row_at = (row // SEG) * (4 * SEG) + turn(member) * SEG + row % SEG
    return key_at <= row_at


def features(projected):
    top = jnp.max(projected, axis=0, keepdims=True)
    bottom = jnp.min(projected, axis=0, keepdims=True)
    plus = jnp.exp(projected - top)
    minus = jnp.exp(bottom - projected)
    plus = plus * (1.0 / jnp.sum(plus, axis=0, keepdims=True))
    minus = minus * (1.0 / jnp.sum(minus, axis=0, keepdims=True))
    return jnp.concatenate([plus, minus], axis=0)


def features_back(phi, grad):
    term = phi * grad
    plus, minus = term[:FD], term[FD:]
    plus = plus - phi[:FD] * jnp.sum(plus, axis=0, keepdims=True)
    minus = minus - phi[FD:] * jnp.sum(minus, axis=0, keepdims=True)
    return plus - minus


def where_is(chunk):
    return (chunk, 0) if chunk < PLACES else (2 * PLACES - 1 - chunk, 1)


def block_rows(refs, block, columns):
    rows = []
    for chunk in range(4 * block, 4 * block + 4):
        place, late = where_is(chunk)
        rows += [ref[place, late, :, columns] for ref in refs]
    return jnp.concatenate(rows, axis=0)


KEY = slice(0, HD)
VALUE = slice(HD, 2 * HD)
QUERY = slice(0, HD)


def pack_kernel(ids_ref, q_ref, k_ref, v_ref, out_ref, outq_ref, flag_ref, ids, q16, wide, k16, v16, sems):
    copies = [
        pltpu.make_async_copy(source, target, sems.at[i])
        for i, (source, target) in enumerate(
            ((ids_ref, ids), (k_ref, k16), (v_ref, v16), (q_ref, q16))
        )
    ]
    for copy in copies:
        copy.start()
    for copy in copies[:3]:
        copy.wait()
    swapped = ids[0] > ids[1]
    flag_ref[0] = jnp.where(swapped, 1, 0)

    def half_rows(late):
        start = jnp.where(swapped, SEG - SEG * late, SEG * late)
        return pl.multiple_of(start, SEG)

    for late in range(2):
        rows = pl.ds(half_rows(late), SEG)
        pair = jnp.concatenate([k16[rows], v16[rows]], axis=1)
        for place in range(PLACES):
            out_ref[place, late] = pair
    copies[3].wait()
    wide[...] = q16[...].astype(F32)
    for late in range(2):
        for place in range(PLACES):
            rows = pl.ds(half_rows(late) * PLACES + place, SEG, stride=PLACES)
            outq_ref[place, late] = wide[rows].astype(BF16)


def tie_kernel(value_ref, token_ref, out_ref):
    pass


def pair_kernel(one_ref, two_ref, out_ref):
    out_ref[...] = (one_ref[...] + two_ref[...]).astype(BF16)


def share_kernel(a_ref, b_ref, c_ref, d_ref, student_ref, out_ref):
    one = a_ref[...].astype(F32) + b_ref[...].astype(F32)
    two = c_ref[...].astype(F32) + d_ref[...].astype(F32)
    total = (one + two).astype(BF16)
    for place in range(PLACES):
        out_ref[place, :2] = student_ref[place]
        out_ref[place, 2] = total


def student_kernel(flag_ref, whole_ref, student_ref, wide):
    swapped = flag_ref[0] == 1
    for late in range(2):
        start = pl.multiple_of(jnp.where(swapped, SEG - SEG * late, SEG * late), SEG)
        for place in range(PLACES):
            rows = pl.ds(start * PLACES + place, SEG, stride=PLACES)
            wide[rows] = whole_ref[place, late].astype(F32)
    student_ref[...] = wide[...].astype(BF16)


def finish_kernel(at_ref, rows_ref, whole_ref, other_ref, student_ref, gq_ref, gk_ref):
    odd = at_ref[1] % 2 == 1
    student_ref[...] = rows_ref[...]
    for place in range(PLACES):
        mine = whole_ref[place, 2].astype(F32)
        other = other_ref[place].astype(F32)
        gq_ref[place] = jnp.where(odd, other, mine)
        gk_ref[place] = jnp.where(odd, mine, other)


def half_forward(refs, masks, queries, phi_q, wk, outs):
    top_ref, total_ref, acc_ref, num_ref, state_ref, phik_ref = outs
    keys, values_t = [], []
    for block in range(BLOCKS):
        keys.append(block_rows(refs, block, KEY))
        value = block_rows(refs, block, VALUE).T
        values_t.append(jnp.concatenate([value, jnp.ones((AUG - HD, HALF), BF16)], axis=0))
    def scores_of(block):
        scores = [dot(keys[b], queries[block], NT) for b in range(block + 1)]
        scores[-1] = jnp.where(masks[block // 2], scores[-1], -1e30)
        top = jnp.max(scores[0], axis=0, keepdims=True)
        for s in scores[1:]:
            top = jnp.maximum(top, jnp.max(s, axis=0, keepdims=True))
        return scores, top

    ready = [scores_of(block) for block in range(BLOCKS)]
    for block in range(BLOCKS):
        scores, top = ready[block]
        total, acc = 0.0, 0.0
        for b, s in enumerate(scores):
            weights = jnp.exp2((s - top) * SCALE)
            total = total + jnp.sum(weights, axis=0, keepdims=True)
            acc = acc + dot(values_t[b][:HD], weights.astype(BF16))
        top_ref[block] = top
        total_ref[block] = total
        acc_ref[block] = acc
    phis = [features(dot(wk, keys[b], NT)) for b in range(BLOCKS)]
    phi16s = [phi.astype(BF16) for phi in phis]
    pairs = [dot(phi16s[b], phi_q[b], (((0,), (0,)), ((), ()))) for b in range(BLOCKS)]
    for b in range(BLOCKS):
        phik_ref[b] = phis[b]
        state_ref[b] = dot(values_t[b], phi16s[b], NT)
    pairs = [jnp.where(masks[b // 2], pairs[b], 0.0) for b in range(BLOCKS)]
    high, low = split(pairs[0])
    num_ref[0] = dot(values_t[0], high) + dot(values_t[0], low)
    for b in range(1, BLOCKS):
        num_ref[b] = dot(values_t[b], pairs[b].astype(BF16))


def first_kernel(at_ref, rows_ref, own_ref, core_ref, wq_ref, wk_ref, phiq_ref, *outs):
    place, member = at_ref[0], at_ref[1]
    masks = [causal_mask(member, (0, 1), late) for late in (False, True)]
    queries = [block_rows((rows_ref,), b, QUERY) for b in range(BLOCKS)]
    phi_q = []
    for block in range(BLOCKS):
        phi = features(dot(wq_ref[place], queries[block], NT))
        phiq_ref[block] = phi
        phi_q.append(phi.astype(BF16))
    half_forward((own_ref, core_ref), masks, queries, phi_q, wk_ref[place], outs)


def second_kernel(
    at_ref, rows_ref, x_ref, far_ref, wk_ref, phiq_ref,
    top_ref, total_ref, acc_ref, num_ref, state_ref,
    student_ref, phik_ref, prior_ref, dn_ref,
    top2_ref, total2_ref, acc2_ref, num2_ref, state2_ref,
):
    place, member = at_ref[0], at_ref[1]
    masks = [causal_mask(member, (2, 3), late) for late in (False, True)]
    queries = [block_rows((rows_ref,), b, QUERY) for b in range(BLOCKS)]
    phi_q = [phiq_ref[block].astype(BF16) for block in range(BLOCKS)]
    outs = (top2_ref, total2_ref, acc2_ref, num2_ref, state2_ref, phik_ref)
    half_forward((x_ref, far_ref), masks, queries, phi_q, wk_ref[place], outs)
    span = range(BLOCKS)
    priors = [None] * BLOCKS
    prior = state_ref[0] + state2_ref[0]
    prior_ref[0] = jnp.zeros((AUG, PHI), F32)
    for b in range(1, BLOCKS):
        priors[b] = prior
        prior_ref[b] = prior
        prior = prior + state_ref[b] + state2_ref[b]
    numerators = [num_ref[b] + num2_ref[b] for b in span]
    for b in range(1, BLOCKS):
        numerators[b] = numerators[b] + dot(priors[b].astype(BF16), phi_q[b])
    teachers = []
    for b in span:
        top = jnp.maximum(top_ref[b], top2_ref[b])
        one = jnp.exp2((top_ref[b] - top) * SCALE)
        two = jnp.exp2((top2_ref[b] - top) * SCALE)
        total = total_ref[b] * one + total2_ref[b] * two
        teachers.append((acc_ref[b] * one + acc2_ref[b] * two) * (1.0 / total))
    inverses = [1.0 / numerators[b][HD:HD + 1] for b in span]
    ys = [numerators[b][:HD] * inverses[b] for b in span]
    index = lax.broadcasted_iota(jnp.int32, (AUG - HD, ROWS), 0)
    for b in span:
        d_num = (ys[b] - teachers[b]) * (inverses[b] * LOSS)
        d_den = -jnp.sum(d_num * ys[b], axis=0, keepdims=True)
        den_high, den_low = split(d_den)
        extra = jnp.where(
            index == 0, den_high.astype(F32), jnp.where(index == 1, den_low.astype(F32), 0.0)
        )
        dn_ref[b] = jnp.concatenate([d_num.astype(BF16), extra.astype(BF16)], axis=0)
    for b in span:
        rows = ys[b].astype(BF16).T
        for i in range(4):
            place, late = where_is(4 * b + i)
            student_ref[place, late] = rows[i * SEG:(i + 1) * SEG]


def backward_kernel(
    at_ref, rows_ref, own_ref, core_ref, x_ref, far_ref, phiq_ref, phik_ref, phik2_ref, prior_ref, dn_ref,
    grad_ref,
):
    member = at_ref[1]
    masks = [
        jnp.concatenate(
            [causal_mask(member, others, late) for others in ((0, 1), (2, 3))], axis=0
        )
        for late in (False, True)
    ]
    pieces = ((own_ref, core_ref), (x_ref, far_ref))

    def both(block, columns):
        return jnp.concatenate([block_rows(refs, block, columns) for refs in pieces], axis=0)

    def project(phi, grad, rows, exact):
        back = features_back(phi, grad)
        if not exact:
            return dot(back.astype(BF16), rows)
        product = dot(jnp.concatenate(split(back), axis=0), rows)
        return product[:FD] + product[FD:]

    span = range(BLOCKS)
    values = [both(b, VALUE) for b in span]
    keys = [both(b, KEY) for b in span]
    queries = [block_rows((rows_ref,), b, QUERY) for b in span]
    phi_q = [phiq_ref[b] for b in span]
    phi_q16 = [p.astype(BF16) for p in phi_q]
    phi_k = [jnp.concatenate([phik_ref[b], phik2_ref[b]], axis=1) for b in span]
    grads = [dn_ref[b] for b in span]
    pairs = []
    for b in span:
        d_den = grads[b][HD:HD + 1].astype(F32) + grads[b][HD + 1:HD + 2].astype(F32)
        pair = dot(values[b], grads[b][:HD]) + d_den
        pairs.append(jnp.where(masks[b // 2], pair, 0.0).astype(BF16))
    terms = [dot(phi_q16[b], grads[b], NT) if b > 0 else None for b in span]
    later = [None] * BLOCKS
    total = terms[3]
    for b in (2, 1, 0):
        later[b] = total
        if b > 0:
            total = total + terms[b]
    grad_phi_q = []
    for b in span:
        if b == 0:
            both_terms = dot(jnp.concatenate(split(phi_k[b]), axis=0), pairs[b])
            grad_phi_q.append(both_terms[:PHI] + both_terms[PHI:])
        else:
            prior = prior_ref[b].T
            grad_phi_q.append(
                dot(phi_k[b].astype(BF16), pairs[b]) + dot(prior.astype(BF16), grads[b])
            )
    grad_phi_k = []
    for b in span:
        if b == BLOCKS - 1:
            grad_phi_k.append(dot(phi_q16[b], pairs[b], NT))
        else:
            grad = dot(
                jnp.concatenate([phi_q16[b], later[b][:, :HD].astype(BF16)], axis=1),
                jnp.concatenate([pairs[b], values[b]], axis=1),
                NT,
            )
            grad_phi_k.append(grad + (later[b][:, HD:HD + 1] + later[b][:, HD + 1:HD + 2]))
    grad_q = project(phi_q[0], grad_phi_q[0], queries[0], True)
    for b in range(1, BLOCKS):
        grad_q = grad_q + project(phi_q[b], grad_phi_q[b], queries[b], False)
    grad_k = project(phi_k[0], grad_phi_k[0], keys[0], True)
    for b in range(1, BLOCKS):
        grad_k = grad_k + project(phi_k[b], grad_phi_k[b], keys[b], False)
    odd = at_ref[1] % 2 == 1
    grad_ref[0] = jnp.where(odd, grad_k, grad_q)
    grad_ref[1] = jnp.where(odd, grad_q, grad_k)


def rest_kernel(
    at_ref, rows_ref, own_ref, core_ref, x_ref, far_ref, wk_ref, phiq_ref,
    top_ref, total_ref, acc_ref, num_ref, state_ref, phik_ref,
    student_ref, grad_ref,
    phik2_ref, prior_ref, dn_ref, *partial,
):
    second_kernel(
        at_ref, rows_ref, x_ref, far_ref, wk_ref, phiq_ref,
        top_ref, total_ref, acc_ref, num_ref, state_ref,
        student_ref, phik2_ref, prior_ref, dn_ref, *partial,
    )
    backward_kernel(
        at_ref, rows_ref, own_ref, core_ref, x_ref, far_ref, phiq_ref, phik_ref, phik2_ref,
        prior_ref, dn_ref, grad_ref,
    )


VMEM = pl.BlockSpec(memory_space=pltpu.VMEM)
SMEM = pl.BlockSpec(memory_space=pltpu.SMEM)
ANY = pl.BlockSpec(memory_space=pl.ANY)
PARAMS = pltpu.CompilerParams(vmem_limit_bytes=8 * 1024 * 1024)
PARTIAL = [
    ((BLOCKS, 1, ROWS), F32),
    ((BLOCKS, 1, ROWS), F32),
    ((BLOCKS, HD, ROWS), F32),
    ((BLOCKS, AUG, ROWS), F32),
    ((BLOCKS, AUG, PHI), F32),
]
PHI_KEYS = ((BLOCKS, PHI, HALF), F32)


def call(kernel, name, outs, args, scratch=(), flops=0, smem=True):
    return pl.pallas_call(
        kernel,
        out_shape=[jax.ShapeDtypeStruct(*out) for out in outs],
        in_specs=[SMEM if smem else VMEM] + [VMEM] * (len(args) - 1),
        out_specs=[VMEM] * len(outs),
        scratch_shapes=[pltpu.VMEM(*s) for s in scratch],
        compiler_params=PARAMS,
        cost_estimate=pl.CostEstimate(flops=flops, bytes_accessed=0, transcendentals=0),
        name=name,
    )(*args)


def tied(array, token):
    return pl.pallas_call(
        tie_kernel,
        out_shape=jax.ShapeDtypeStruct(array.shape, array.dtype),
        in_specs=[ANY, ANY],
        out_specs=ANY,
        input_output_aliases={0: 0},
        compiler_params=pltpu.CompilerParams(vmem_limit_bytes=1024 * 1024),
        name="tie",
    )(array, token)


def on_device(queries, keys, values, segment_ids, feat_query, feat_key):
    spot = lax.axis_index("ctx")
    place, member = spot // MEMBERS, spot % MEMBERS
    z_groups = [[j + MEMBERS * k for k in range(PLACES)] for j in range(MEMBERS)]

    def swap(array, relative):
        return lax.ppermute(array, "ctx", [(i, i ^ relative) for i in range(32)])

    def along_z(array):
        return lax.all_to_all(array, "ctx", 0, 0, axis_index_groups=z_groups)

    at = jnp.stack([place, member]).astype(jnp.int32)

    sent, sent_q, flag = pl.pallas_call(
        pack_kernel,
        out_shape=[
            jax.ShapeDtypeStruct((PLACES, 2, SEG, 2 * HD), BF16),
            jax.ShapeDtypeStruct((PLACES, 2, SEG, HD), BF16),
            jax.ShapeDtypeStruct((1,), jnp.int32),
        ],
        in_specs=[ANY] * 4,
        out_specs=[VMEM, VMEM, SMEM],
        scratch_shapes=[
            pltpu.SMEM((2,), jnp.int32),
            pltpu.VMEM((2 * SEG * PLACES, HD), BF16),
            pltpu.VMEM((2 * SEG * PLACES, HD), F32),
            pltpu.VMEM((2 * SEG, HD), BF16),
            pltpu.VMEM((2 * SEG, HD), BF16),
            pltpu.SemaphoreType.DMA((4,)),
        ],
        compiler_params=pltpu.CompilerParams(vmem_limit_bytes=62 * 1024 * 1024),
        name="pack",
    )(
        segment_ids,
        queries.reshape(2 * SEG * PLACES, HD),
        keys.reshape(2 * SEG, HD),
        values.reshape(2 * SEG, HD),
    )
    own = along_z(sent)
    beside = swap(own, 2)
    core = swap(own, 1)
    rows = along_z(tied(sent_q, own))

    wq = jnp.transpose(feat_query, (0, 2, 1))
    wk = jnp.transpose(feat_key, (0, 2, 1))

    phi_q, *first = call(
        first_kernel, "first_half",
        [((BLOCKS, PHI, ROWS), F32)] + PARTIAL + [PHI_KEYS],
        (at, rows, own, core, wq, wk),
        flops=5 * 10 ** 9,
    )
    beside = tied(beside, rows)
    far = swap(beside, 1)
    student, grad = call(
        rest_kernel, "rest",
        [((PLACES, 2, SEG, HD), BF16), ((2, FD, HD), F32)],
        (at, rows, own, core, beside, far, wk, phi_q, *first),
        [PHI_KEYS, ((BLOCKS, AUG, PHI), F32), ((BLOCKS, AUG, ROWS), BF16)] + PARTIAL,
        flops=10 ** 10,
    )
    def swap_wide(array, relative):
        pairs = [(i, i ^ relative) for i in range(64)]
        return lax.ppermute(array, ("dp", "ctx"), pairs)

    (pair,) = call(
        pair_kernel, "pair", [((FD, HD), BF16)], (grad[0], swap(grad[1], 1)), smem=False
    )
    (share,) = call(
        share_kernel, "share", [((PLACES, 3, SEG, HD), BF16)],
        (pair, swap_wide(pair, 2), swap_wide(pair, 32), swap_wide(pair, 34), student),
        smem=False,
    )
    whole = along_z(share)
    other = swap(whole[:, 2], 1)
    (student,) = call(
        student_kernel, "student_rows", [((2 * SEG * PLACES, HD), BF16)], (flag, whole),
        [((2 * SEG * PLACES, HD), F32)],
    )
    student, grad_query, grad_key = call(
        finish_kernel, "finish",
        [((2 * SEG * PLACES, HD), BF16)] + [((PLACES, FD, HD), F32)] * 2,
        (at, student, whole, other),
    )
    student = student.reshape(2 * SEG, 1, PLACES, HD)
    return student, jnp.transpose(grad_query, (0, 2, 1)), jnp.transpose(grad_key, (0, 2, 1))


def solution(mesh):
    placed = (
        P("ctx", "dp", "tensor", None),
        P("ctx", "dp", "tensor", None),
        P("ctx", "dp", "tensor", None),
        P("ctx"),
        P("tensor", None, None),
        P("tensor", None, None),
    )
    return jax.shard_map(
        on_device,
        mesh=mesh,
        in_specs=placed,
        out_specs=(
            P("ctx", "dp", "tensor", None),
            P("tensor", None, None),
            P("tensor", None, None),
        ),
        check_vma=False,
    )
```

```python
import math

import jax
import jax.numpy as jnp
from jax import lax
from jax.experimental import pallas as pl
from jax.experimental.pallas import tpu as pltpu
from jax.sharding import PartitionSpec as P

PLACES = 8
MEMBERS = 4
ORDER = (0, 2, 4, 6, 1, 3, 5, 7)
SLOT = tuple(ORDER.index(place) for place in range(PLACES))
SEG = 64
HD = 128
FD = 64
PHI = 2 * FD
BLOCKS = 4
ROWS = 4 * SEG
HALF = 8 * SEG
AUG = HD + 16
LOSS = 1.0 / 8192.0
SCALE = (HD ** -0.5) * math.log2(math.e)
F32 = jnp.float32
BF16 = jnp.bfloat16
NN = (((1,), (0,)), ((), ()))
NT = (((1,), (1,)), ((), ()))


def dot(a, b, dims=NN):
    return lax.dot_general(a, b, dims, preferred_element_type=F32)


def split(array):
    high = array.astype(BF16)
    return high, (array - high.astype(F32)).astype(BF16)


def causal_mask(member, others, late):
    def turn(who):
        return 3 - who if late else who

    key = lax.broadcasted_iota(jnp.int32, (HALF, 1), 0)
    row = lax.broadcasted_iota(jnp.int32, (1, ROWS), 1)
    second = (key // SEG) % 2
    who = jnp.where(second == 0, member ^ others[0], member ^ others[1])
    key_at = (key // (2 * SEG)) * (4 * SEG) + turn(who) * SEG + key % SEG
    row_at = (row // SEG) * (4 * SEG) + turn(member) * SEG + row % SEG
    return key_at <= row_at


def features(projected):
    top = jnp.max(projected, axis=0, keepdims=True)
    bottom = jnp.min(projected, axis=0, keepdims=True)
    plus = jnp.exp(projected - top)
    minus = jnp.exp(bottom - projected)
    plus = plus * (1.0 / jnp.sum(plus, axis=0, keepdims=True))
    minus = minus * (1.0 / jnp.sum(minus, axis=0, keepdims=True))
    return jnp.concatenate([plus, minus], axis=0)


def features_back(phi, grad):
    term = phi * grad
    plus, minus = term[:FD], term[FD:]
    plus = plus - phi[:FD] * jnp.sum(plus, axis=0, keepdims=True)
    minus = minus - phi[FD:] * jnp.sum(minus, axis=0, keepdims=True)
    return plus - minus


def where_is(chunk):
    return (SLOT[chunk], 0) if chunk < PLACES else (SLOT[2 * PLACES - 1 - chunk], 1)


def block_rows(refs, block, columns):
    rows = []
    for chunk in range(4 * block, 4 * block + 4):
        place, late = where_is(chunk)
        rows += [ref[place, late, :, columns] for ref in refs]
    return jnp.concatenate(rows, axis=0)


KEY = slice(0, HD)
VALUE = slice(HD, 2 * HD)
QUERY = slice(0, HD)


def pack_kernel(ids_ref, q_ref, k_ref, v_ref, out_ref, outq_ref, flag_ref, ids, q16, wide, k16, v16, sems):
    copies = [
        pltpu.make_async_copy(source, target, sems.at[i])
        for i, (source, target) in enumerate(
            ((ids_ref, ids), (k_ref, k16), (v_ref, v16), (q_ref, q16))
        )
    ]
    for copy in copies:
        copy.start()
    for copy in copies[:3]:
        copy.wait()
    swapped = ids[0] > ids[1]
    flag_ref[0] = jnp.where(swapped, 1, 0)

    def half_rows(late):
        start = jnp.where(swapped, SEG - SEG * late, SEG * late)
        return pl.multiple_of(start, SEG)

    for late in range(2):
        rows = pl.ds(half_rows(late), SEG)
        pair = jnp.concatenate([k16[rows], v16[rows]], axis=1)
        for place in range(PLACES):
            out_ref[place, late] = pair
    copies[3].wait()
    wide[...] = q16[...].astype(F32)
    for late in range(2):
        for place in range(PLACES):
            rows = pl.ds(half_rows(late) * PLACES + place, SEG, stride=PLACES)
            outq_ref[SLOT[place], late] = wide[rows].astype(BF16)


def tie_kernel(value_ref, token_ref, out_ref):
    pass


def pair_kernel(one_ref, two_ref, out_ref):
    out_ref[...] = (one_ref[...] + two_ref[...]).astype(BF16)


def share_kernel(a_ref, b_ref, c_ref, d_ref, student_ref, out_ref):
    one = a_ref[...].astype(F32) + b_ref[...].astype(F32)
    two = c_ref[...].astype(F32) + d_ref[...].astype(F32)
    total = (one + two).astype(BF16)
    for place in range(PLACES):
        out_ref[place, :2] = student_ref[place]
        out_ref[place, 2] = total


def student_kernel(flag_ref, whole_ref, student_ref, wide):
    swapped = flag_ref[0] == 1
    for late in range(2):
        start = pl.multiple_of(jnp.where(swapped, SEG - SEG * late, SEG * late), SEG)
        for place in range(PLACES):
            rows = pl.ds(start * PLACES + place, SEG, stride=PLACES)
            wide[rows] = whole_ref[SLOT[place], late].astype(F32)
    student_ref[...] = wide[...].astype(BF16)


def finish_kernel(at_ref, rows_ref, whole_ref, other_ref, student_ref, gq_ref, gk_ref):
    odd = at_ref[1] % 2 == 1
    student_ref[...] = rows_ref[...]
    for place in range(PLACES):
        mine = whole_ref[SLOT[place], 2].astype(F32)
        other = other_ref[SLOT[place]].astype(F32)
        gq_ref[place] = jnp.where(odd, other, mine)
        gk_ref[place] = jnp.where(odd, mine, other)


def half_forward(refs, masks, queries, phi_q, wk, outs):
    top_ref, total_ref, acc_ref, num_ref, state_ref, phik_ref = outs
    keys, values_t = [], []
    for block in range(BLOCKS):
        keys.append(block_rows(refs, block, KEY))
        value = block_rows(refs, block, VALUE).T
        values_t.append(jnp.concatenate([value, jnp.ones((AUG - HD, HALF), BF16)], axis=0))
    def scores_of(block):
        scores = [dot(keys[b], queries[block], NT) for b in range(block + 1)]
        scores[-1] = jnp.where(masks[block // 2], scores[-1], -1e30)
        top = jnp.max(scores[0], axis=0, keepdims=True)
        for s in scores[1:]:
            top = jnp.maximum(top, jnp.max(s, axis=0, keepdims=True))
        return scores, top

    ready = [scores_of(block) for block in range(BLOCKS)]
    for block in range(BLOCKS):
        scores, top = ready[block]
        total, acc = 0.0, 0.0
        for b, s in enumerate(scores):
            weights = jnp.exp2((s - top) * SCALE)
            total = total + jnp.sum(weights, axis=0, keepdims=True)
            acc = acc + dot(values_t[b][:HD], weights.astype(BF16))
        top_ref[block] = top
        total_ref[block] = total
        acc_ref[block] = acc
    phis = [features(dot(wk, keys[b], NT)) for b in range(BLOCKS)]
    phi16s = [phi.astype(BF16) for phi in phis]
    pairs = [dot(phi16s[b], phi_q[b], (((0,), (0,)), ((), ()))) for b in range(BLOCKS)]
    for b in range(BLOCKS):
        phik_ref[b] = phis[b]
        state_ref[b] = dot(values_t[b], phi16s[b], NT)
    pairs = [jnp.where(masks[b // 2], pairs[b], 0.0) for b in range(BLOCKS)]
    high, low = split(pairs[0])
    num_ref[0] = dot(values_t[0], high) + dot(values_t[0], low)
    for b in range(1, BLOCKS):
        num_ref[b] = dot(values_t[b], pairs[b].astype(BF16))


def first_kernel(at_ref, rows_ref, own_ref, core_ref, wq_ref, wk_ref, phiq_ref, *outs):
    place, member = at_ref[0], at_ref[1]
    masks = [causal_mask(member, (0, 1), late) for late in (False, True)]
    queries = [block_rows((rows_ref,), b, QUERY) for b in range(BLOCKS)]
    phi_q = []
    for block in range(BLOCKS):
        phi = features(dot(wq_ref[place], queries[block], NT))
        phiq_ref[block] = phi
        phi_q.append(phi.astype(BF16))
    half_forward((own_ref, core_ref), masks, queries, phi_q, wk_ref[place], outs)


def second_kernel(
    at_ref, rows_ref, x_ref, far_ref, wk_ref, phiq_ref,
    top_ref, total_ref, acc_ref, num_ref, state_ref,
    student_ref, phik_ref, prior_ref, dn_ref,
    top2_ref, total2_ref, acc2_ref, num2_ref, state2_ref,
):
    place, member = at_ref[0], at_ref[1]
    masks = [causal_mask(member, (2, 3), late) for late in (False, True)]
    queries = [block_rows((rows_ref,), b, QUERY) for b in range(BLOCKS)]
    phi_q = [phiq_ref[block].astype(BF16) for block in range(BLOCKS)]
    outs = (top2_ref, total2_ref, acc2_ref, num2_ref, state2_ref, phik_ref)
    half_forward((x_ref, far_ref), masks, queries, phi_q, wk_ref[place], outs)
    span = range(BLOCKS)
    priors = [None] * BLOCKS
    prior = state_ref[0] + state2_ref[0]
    prior_ref[0] = jnp.zeros((AUG, PHI), F32)
    for b in range(1, BLOCKS):
        priors[b] = prior
        prior_ref[b] = prior
        prior = prior + state_ref[b] + state2_ref[b]
    numerators = [num_ref[b] + num2_ref[b] for b in span]
    for b in range(1, BLOCKS):
        numerators[b] = numerators[b] + dot(priors[b].astype(BF16), phi_q[b])
    teachers = []
    for b in span:
        top = jnp.maximum(top_ref[b], top2_ref[b])
        one = jnp.exp2((top_ref[b] - top) * SCALE)
        two = jnp.exp2((top2_ref[b] - top) * SCALE)
        total = total_ref[b] * one + total2_ref[b] * two
        teachers.append((acc_ref[b] * one + acc2_ref[b] * two) * (1.0 / total))
    inverses = [1.0 / numerators[b][HD:HD + 1] for b in span]
    ys = [numerators[b][:HD] * inverses[b] for b in span]
    index = lax.broadcasted_iota(jnp.int32, (AUG - HD, ROWS), 0)
    for b in span:
        d_num = (ys[b] - teachers[b]) * (inverses[b] * LOSS)
        d_den = -jnp.sum(d_num * ys[b], axis=0, keepdims=True)
        den_high, den_low = split(d_den)
        extra = jnp.where(
            index == 0, den_high.astype(F32), jnp.where(index == 1, den_low.astype(F32), 0.0)
        )
        dn_ref[b] = jnp.concatenate([d_num.astype(BF16), extra.astype(BF16)], axis=0)
    for b in span:
        rows = ys[b].astype(BF16).T
        for i in range(4):
            place, late = where_is(4 * b + i)
            student_ref[place, late] = rows[i * SEG:(i + 1) * SEG]


def backward_kernel(
    at_ref, rows_ref, own_ref, core_ref, x_ref, far_ref, phiq_ref, phik_ref, phik2_ref, prior_ref, dn_ref,
    grad_ref,
):
    member = at_ref[1]
    masks = [
        jnp.concatenate(
            [causal_mask(member, others, late) for others in ((0, 1), (2, 3))], axis=0
        )
        for late in (False, True)
    ]
    pieces = ((own_ref, core_ref), (x_ref, far_ref))

    def both(block, columns):
        return jnp.concatenate([block_rows(refs, block, columns) for refs in pieces], axis=0)

    def project(phi, grad, rows, exact):
        back = features_back(phi, grad)
        if not exact:
            return dot(back.astype(BF16), rows)
        product = dot(jnp.concatenate(split(back), axis=0), rows)
        return product[:FD] + product[FD:]

    span = range(BLOCKS)
    values = [both(b, VALUE) for b in span]
    keys = [both(b, KEY) for b in span]
    queries = [block_rows((rows_ref,), b, QUERY) for b in span]
    phi_q = [phiq_ref[b] for b in span]
    phi_q16 = [p.astype(BF16) for p in phi_q]
    phi_k = [jnp.concatenate([phik_ref[b], phik2_ref[b]], axis=1) for b in span]
    grads = [dn_ref[b] for b in span]
    pairs = []
    for b in span:
        d_den = grads[b][HD:HD + 1].astype(F32) + grads[b][HD + 1:HD + 2].astype(F32)
        pair = dot(values[b], grads[b][:HD]) + d_den
        pairs.append(jnp.where(masks[b // 2], pair, 0.0).astype(BF16))
    terms = [dot(phi_q16[b], grads[b], NT) if b > 0 else None for b in span]
    later = [None] * BLOCKS
    total = terms[3]
    for b in (2, 1, 0):
        later[b] = total
        if b > 0:
            total = total + terms[b]
    grad_phi_q = []
    for b in span:
        if b == 0:
            both_terms = dot(jnp.concatenate(split(phi_k[b]), axis=0), pairs[b])
            grad_phi_q.append(both_terms[:PHI] + both_terms[PHI:])
        else:
            prior = prior_ref[b].T
            grad_phi_q.append(
                dot(phi_k[b].astype(BF16), pairs[b]) + dot(prior.astype(BF16), grads[b])
            )
    grad_phi_k = []
    for b in span:
        if b == BLOCKS - 1:
            grad_phi_k.append(dot(phi_q16[b], pairs[b], NT))
        else:
            grad = dot(
                jnp.concatenate([phi_q16[b], later[b][:, :HD].astype(BF16)], axis=1),
                jnp.concatenate([pairs[b], values[b]], axis=1),
                NT,
            )
            grad_phi_k.append(grad + (later[b][:, HD:HD + 1] + later[b][:, HD + 1:HD + 2]))
    grad_q = project(phi_q[0], grad_phi_q[0], queries[0], True)
    for b in range(1, BLOCKS):
        grad_q = grad_q + project(phi_q[b], grad_phi_q[b], queries[b], False)
    grad_k = project(phi_k[0], grad_phi_k[0], keys[0], True)
    for b in range(1, BLOCKS):
        grad_k = grad_k + project(phi_k[b], grad_phi_k[b], keys[b], False)
    odd = at_ref[1] % 2 == 1
    grad_ref[0] = jnp.where(odd, grad_k, grad_q)
    grad_ref[1] = jnp.where(odd, grad_q, grad_k)


def rest_kernel(
    at_ref, rows_ref, own_ref, core_ref, x_ref, far_ref, wk_ref, phiq_ref,
    top_ref, total_ref, acc_ref, num_ref, state_ref, phik_ref,
    student_ref, grad_ref,
    phik2_ref, prior_ref, dn_ref, *partial,
):
    second_kernel(
        at_ref, rows_ref, x_ref, far_ref, wk_ref, phiq_ref,
        top_ref, total_ref, acc_ref, num_ref, state_ref,
        student_ref, phik2_ref, prior_ref, dn_ref, *partial,
    )
    backward_kernel(
        at_ref, rows_ref, own_ref, core_ref, x_ref, far_ref, phiq_ref, phik_ref, phik2_ref,
        prior_ref, dn_ref, grad_ref,
    )


VMEM = pl.BlockSpec(memory_space=pltpu.VMEM)
SMEM = pl.BlockSpec(memory_space=pltpu.SMEM)
ANY = pl.BlockSpec(memory_space=pl.ANY)
PARAMS = pltpu.CompilerParams(vmem_limit_bytes=8 * 1024 * 1024)
PARTIAL = [
    ((BLOCKS, 1, ROWS), F32),
    ((BLOCKS, 1, ROWS), F32),
    ((BLOCKS, HD, ROWS), F32),
    ((BLOCKS, AUG, ROWS), F32),
    ((BLOCKS, AUG, PHI), F32),
]
PHI_KEYS = ((BLOCKS, PHI, HALF), F32)


def call(kernel, name, outs, args, scratch=(), flops=0, smem=True):
    return pl.pallas_call(
        kernel,
        out_shape=[jax.ShapeDtypeStruct(*out) for out in outs],
        in_specs=[SMEM if smem else VMEM] + [VMEM] * (len(args) - 1),
        out_specs=[VMEM] * len(outs),
        scratch_shapes=[pltpu.VMEM(*s) for s in scratch],
        compiler_params=PARAMS,
        cost_estimate=pl.CostEstimate(flops=flops, bytes_accessed=0, transcendentals=0),
        name=name,
    )(*args)


def tied(array, token):
    return pl.pallas_call(
        tie_kernel,
        out_shape=jax.ShapeDtypeStruct(array.shape, array.dtype),
        in_specs=[ANY, ANY],
        out_specs=ANY,
        input_output_aliases={0: 0},
        compiler_params=pltpu.CompilerParams(vmem_limit_bytes=1024 * 1024),
        name="tie",
    )(array, token)


def on_device(queries, keys, values, segment_ids, feat_query, feat_key):
    spot = lax.axis_index("ctx")
    place, member = spot // MEMBERS, spot % MEMBERS
    z_groups = [[j + MEMBERS * k for k in ORDER] for j in range(MEMBERS)]

    def swap(array, relative):
        return lax.ppermute(array, "ctx", [(i, i ^ relative) for i in range(32)])

    def along_z(array):
        return lax.all_to_all(array, "ctx", 0, 0, axis_index_groups=z_groups)

    at = jnp.stack([place, member]).astype(jnp.int32)

    sent, sent_q, flag = pl.pallas_call(
        pack_kernel,
        out_shape=[
            jax.ShapeDtypeStruct((PLACES, 2, SEG, 2 * HD), BF16),
            jax.ShapeDtypeStruct((PLACES, 2, SEG, HD), BF16),
            jax.ShapeDtypeStruct((1,), jnp.int32),
        ],
        in_specs=[ANY] * 4,
        out_specs=[VMEM, VMEM, SMEM],
        scratch_shapes=[
            pltpu.SMEM((2,), jnp.int32),
            pltpu.VMEM((2 * SEG * PLACES, HD), BF16),
            pltpu.VMEM((2 * SEG * PLACES, HD), F32),
            pltpu.VMEM((2 * SEG, HD), BF16),
            pltpu.VMEM((2 * SEG, HD), BF16),
            pltpu.SemaphoreType.DMA((4,)),
        ],
        compiler_params=pltpu.CompilerParams(vmem_limit_bytes=62 * 1024 * 1024),
        name="pack",
    )(
        segment_ids,
        queries.reshape(2 * SEG * PLACES, HD),
        keys.reshape(2 * SEG, HD),
        values.reshape(2 * SEG, HD),
    )
    own = along_z(sent)
    beside = swap(own, 2)
    core = swap(own, 1)
    rows = along_z(tied(sent_q, own))

    wq = jnp.transpose(feat_query, (0, 2, 1))
    wk = jnp.transpose(feat_key, (0, 2, 1))

    phi_q, *first = call(
        first_kernel, "first_half",
        [((BLOCKS, PHI, ROWS), F32)] + PARTIAL + [PHI_KEYS],
        (at, rows, own, core, wq, wk),
        flops=5 * 10 ** 9,
    )
    beside = tied(beside, rows)
    far = swap(beside, 1)
    student, grad = call(
        rest_kernel, "rest",
        [((PLACES, 2, SEG, HD), BF16), ((2, FD, HD), F32)],
        (at, rows, own, core, beside, far, wk, phi_q, *first),
        [PHI_KEYS, ((BLOCKS, AUG, PHI), F32), ((BLOCKS, AUG, ROWS), BF16)] + PARTIAL,
        flops=10 ** 10,
    )
    def swap_wide(array, relative):
        pairs = [(i, i ^ relative) for i in range(64)]
        return lax.ppermute(array, ("dp", "ctx"), pairs)

    (pair,) = call(
        pair_kernel, "pair", [((FD, HD), BF16)], (grad[0], swap(grad[1], 1)), smem=False
    )
    (share,) = call(
        share_kernel, "share", [((PLACES, 3, SEG, HD), BF16)],
        (pair, swap_wide(pair, 2), swap_wide(pair, 32), swap_wide(pair, 34), student),
        smem=False,
    )
    whole = along_z(share)
    other = swap(whole[:, 2], 1)
    (student,) = call(
        student_kernel, "student_rows", [((2 * SEG * PLACES, HD), BF16)], (flag, whole),
        [((2 * SEG * PLACES, HD), F32)],
    )
    student, grad_query, grad_key = call(
        finish_kernel, "finish",
        [((2 * SEG * PLACES, HD), BF16)] + [((PLACES, FD, HD), F32)] * 2,
        (at, student, whole, other),
    )
    student = student.reshape(2 * SEG, 1, PLACES, HD)
    return student, jnp.transpose(grad_query, (0, 2, 1)), jnp.transpose(grad_key, (0, 2, 1))


def solution(mesh):
    placed = (
        P("ctx", "dp", "tensor", None),
        P("ctx", "dp", "tensor", None),
        P("ctx", "dp", "tensor", None),
        P("ctx"),
        P("tensor", None, None),
        P("tensor", None, None),
    )
    return jax.shard_map(
        on_device,
        mesh=mesh,
        in_specs=placed,
        out_specs=(
            P("ctx", "dp", "tensor", None),
            P("tensor", None, None),
            P("tensor", None, None),
        ),
        check_vma=False,
    )
```

```python
import math

import jax
import jax.numpy as jnp
from jax import lax
from jax.experimental import pallas as pl
from jax.experimental.pallas import tpu as pltpu
from jax.sharding import PartitionSpec as P

PLACES = 8
MEMBERS = 4
ORDER = (0, 2, 4, 6, 7, 1, 3, 5)
SLOT = tuple(ORDER.index(place) for place in range(PLACES))
SEG = 64
HD = 128
FD = 64
PHI = 2 * FD
BLOCKS = 4
ROWS = 4 * SEG
HALF = 8 * SEG
AUG = HD + 16
LOSS = 1.0 / 8192.0
SCALE = (HD ** -0.5) * math.log2(math.e)
F32 = jnp.float32
BF16 = jnp.bfloat16
NN = (((1,), (0,)), ((), ()))
NT = (((1,), (1,)), ((), ()))


def dot(a, b, dims=NN):
    return lax.dot_general(a, b, dims, preferred_element_type=F32)


def split(array):
    high = array.astype(BF16)
    return high, (array - high.astype(F32)).astype(BF16)


def causal_mask(member, others, late):
    def turn(who):
        return 3 - who if late else who

    key = lax.broadcasted_iota(jnp.int32, (HALF, 1), 0)
    row = lax.broadcasted_iota(jnp.int32, (1, ROWS), 1)
    second = (key // SEG) % 2
    who = jnp.where(second == 0, member ^ others[0], member ^ others[1])
    key_at = (key // (2 * SEG)) * (4 * SEG) + turn(who) * SEG + key % SEG
    row_at = (row // SEG) * (4 * SEG) + turn(member) * SEG + row % SEG
    return key_at <= row_at


def features(projected):
    top = jnp.max(projected, axis=0, keepdims=True)
    bottom = jnp.min(projected, axis=0, keepdims=True)
    plus = jnp.exp(projected - top)
    minus = jnp.exp(bottom - projected)
    plus = plus * (1.0 / jnp.sum(plus, axis=0, keepdims=True))
    minus = minus * (1.0 / jnp.sum(minus, axis=0, keepdims=True))
    return jnp.concatenate([plus, minus], axis=0)


def features_back(phi, grad):
    term = phi * grad
    plus, minus = term[:FD], term[FD:]
    plus = plus - phi[:FD] * jnp.sum(plus, axis=0, keepdims=True)
    minus = minus - phi[FD:] * jnp.sum(minus, axis=0, keepdims=True)
    return plus - minus


def where_is(chunk):
    return (SLOT[chunk], 0) if chunk < PLACES else (SLOT[2 * PLACES - 1 - chunk], 1)


def block_rows(refs, block, columns):
    rows = []
    for chunk in range(4 * block, 4 * block + 4):
        place, late = where_is(chunk)
        rows += [ref[place, late, :, columns] for ref in refs]
    return jnp.concatenate(rows, axis=0)


KEY = slice(0, HD)
VALUE = slice(HD, 2 * HD)
QUERY = slice(0, HD)


def pack_kernel(ids_ref, q_ref, k_ref, v_ref, out_ref, outq_ref, flag_ref, ids, q16, wide, k16, v16, sems):
    copies = [
        pltpu.make_async_copy(source, target, sems.at[i])
        for i, (source, target) in enumerate(
            ((ids_ref, ids), (k_ref, k16), (v_ref, v16), (q_ref, q16))
        )
    ]
    for copy in copies:
        copy.start()
    for copy in copies[:3]:
        copy.wait()
    swapped = ids[0] > ids[1]
    flag_ref[0] = jnp.where(swapped, 1, 0)

    def half_rows(late):
        start = jnp.where(swapped, SEG - SEG * late, SEG * late)
        return pl.multiple_of(start, SEG)

    for late in range(2):
        rows = pl.ds(half_rows(late), SEG)
        pair = jnp.concatenate([k16[rows], v16[rows]], axis=1)
        for place in range(PLACES):
            out_ref[place, late] = pair
    copies[3].wait()
    wide[...] = q16[...].astype(F32)
    for late in range(2):
        for place in range(PLACES):
            rows = pl.ds(half_rows(late) * PLACES + place, SEG, stride=PLACES)
            outq_ref[SLOT[place], late] = wide[rows].astype(BF16)


def tie_kernel(value_ref, token_ref, out_ref):
    pass


def pair_kernel(one_ref, two_ref, out_ref):
    out_ref[...] = (one_ref[...] + two_ref[...]).astype(BF16)


def share_kernel(a_ref, b_ref, c_ref, d_ref, student_ref, out_ref):
    one = a_ref[...].astype(F32) + b_ref[...].astype(F32)
    two = c_ref[...].astype(F32) + d_ref[...].astype(F32)
    total = (one + two).astype(BF16)
    for place in range(PLACES):
        out_ref[place, :2] = student_ref[place]
        out_ref[place, 2] = total


def student_kernel(flag_ref, whole_ref, student_ref, wide):
    swapped = flag_ref[0] == 1
    for late in range(2):
        start = pl.multiple_of(jnp.where(swapped, SEG - SEG * late, SEG * late), SEG)
        for place in range(PLACES):
            rows = pl.ds(start * PLACES + place, SEG, stride=PLACES)
            wide[rows] = whole_ref[SLOT[place], late].astype(F32)
    student_ref[...] = wide[...].astype(BF16)


def finish_kernel(at_ref, rows_ref, whole_ref, other_ref, student_ref, gq_ref, gk_ref):
    odd = at_ref[1] % 2 == 1
    student_ref[...] = rows_ref[...]
    for place in range(PLACES):
        mine = whole_ref[SLOT[place], 2].astype(F32)
        other = other_ref[SLOT[place]].astype(F32)
        gq_ref[place] = jnp.where(odd, other, mine)
        gk_ref[place] = jnp.where(odd, mine, other)


def half_forward(refs, masks, queries, phi_q, wk, outs):
    top_ref, total_ref, acc_ref, num_ref, state_ref, phik_ref = outs
    keys, values_t = [], []
    for block in range(BLOCKS):
        keys.append(block_rows(refs, block, KEY))
        value = block_rows(refs, block, VALUE).T
        values_t.append(jnp.concatenate([value, jnp.ones((AUG - HD, HALF), BF16)], axis=0))
    def scores_of(block):
        scores = [dot(keys[b], queries[block], NT) for b in range(block + 1)]
        scores[-1] = jnp.where(masks[block // 2], scores[-1], -1e30)
        top = jnp.max(scores[0], axis=0, keepdims=True)
        for s in scores[1:]:
            top = jnp.maximum(top, jnp.max(s, axis=0, keepdims=True))
        return scores, top

    ready = [scores_of(block) for block in range(BLOCKS)]
    for block in range(BLOCKS):
        scores, top = ready[block]
        total, acc = 0.0, 0.0
        for b, s in enumerate(scores):
            weights = jnp.exp2((s - top) * SCALE)
            total = total + jnp.sum(weights, axis=0, keepdims=True)
            acc = acc + dot(values_t[b][:HD], weights.astype(BF16))
        top_ref[block] = top
        total_ref[block] = total
        acc_ref[block] = acc
    phis = [features(dot(wk, keys[b], NT)) for b in range(BLOCKS)]
    phi16s = [phi.astype(BF16) for phi in phis]
    pairs = [dot(phi16s[b], phi_q[b], (((0,), (0,)), ((), ()))) for b in range(BLOCKS)]
    for b in range(BLOCKS):
        phik_ref[b] = phis[b]
        state_ref[b] = dot(values_t[b], phi16s[b], NT)
    pairs = [jnp.where(masks[b // 2], pairs[b], 0.0) for b in range(BLOCKS)]
    high, low = split(pairs[0])
    num_ref[0] = dot(values_t[0], high) + dot(values_t[0], low)
    for b in range(1, BLOCKS):
        num_ref[b] = dot(values_t[b], pairs[b].astype(BF16))


def first_kernel(at_ref, rows_ref, own_ref, core_ref, wq_ref, wk_ref, phiq_ref, *outs):
    place, member = at_ref[0], at_ref[1]
    masks = [causal_mask(member, (0, 1), late) for late in (False, True)]
    queries = [block_rows((rows_ref,), b, QUERY) for b in range(BLOCKS)]
    phi_q = []
    for block in range(BLOCKS):
        phi = features(dot(wq_ref[place], queries[block], NT))
        phiq_ref[block] = phi
        phi_q.append(phi.astype(BF16))
    half_forward((own_ref, core_ref), masks, queries, phi_q, wk_ref[place], outs)


def second_kernel(
    at_ref, rows_ref, x_ref, far_ref, wk_ref, phiq_ref,
    top_ref, total_ref, acc_ref, num_ref, state_ref,
    student_ref, phik_ref, prior_ref, dn_ref,
    top2_ref, total2_ref, acc2_ref, num2_ref, state2_ref,
):
    place, member = at_ref[0], at_ref[1]
    masks = [causal_mask(member, (2, 3), late) for late in (False, True)]
    queries = [block_rows((rows_ref,), b, QUERY) for b in range(BLOCKS)]
    phi_q = [phiq_ref[block].astype(BF16) for block in range(BLOCKS)]
    outs = (top2_ref, total2_ref, acc2_ref, num2_ref, state2_ref, phik_ref)
    half_forward((x_ref, far_ref), masks, queries, phi_q, wk_ref[place], outs)
    span = range(BLOCKS)
    priors = [None] * BLOCKS
    prior = state_ref[0] + state2_ref[0]
    prior_ref[0] = jnp.zeros((AUG, PHI), F32)
    for b in range(1, BLOCKS):
        priors[b] = prior
        prior_ref[b] = prior
        prior = prior + state_ref[b] + state2_ref[b]
    numerators = [num_ref[b] + num2_ref[b] for b in span]
    for b in range(1, BLOCKS):
        numerators[b] = numerators[b] + dot(priors[b].astype(BF16), phi_q[b])
    teachers = []
    for b in span:
        top = jnp.maximum(top_ref[b], top2_ref[b])
        one = jnp.exp2((top_ref[b] - top) * SCALE)
        two = jnp.exp2((top2_ref[b] - top) * SCALE)
        total = total_ref[b] * one + total2_ref[b] * two
        teachers.append((acc_ref[b] * one + acc2_ref[b] * two) * (1.0 / total))
    inverses = [1.0 / numerators[b][HD:HD + 1] for b in span]
    ys = [numerators[b][:HD] * inverses[b] for b in span]
    index = lax.broadcasted_iota(jnp.int32, (AUG - HD, ROWS), 0)
    for b in span:
        d_num = (ys[b] - teachers[b]) * (inverses[b] * LOSS)
        d_den = -jnp.sum(d_num * ys[b], axis=0, keepdims=True)
        den_high, den_low = split(d_den)
        extra = jnp.where(
            index == 0, den_high.astype(F32), jnp.where(index == 1, den_low.astype(F32), 0.0)
        )
        dn_ref[b] = jnp.concatenate([d_num.astype(BF16), extra.astype(BF16)], axis=0)
    for b in span:
        rows = ys[b].astype(BF16).T
        for i in range(4):
            place, late = where_is(4 * b + i)
            student_ref[place, late] = rows[i * SEG:(i + 1) * SEG]


def backward_kernel(
    at_ref, rows_ref, own_ref, core_ref, x_ref, far_ref, phiq_ref, phik_ref, phik2_ref, prior_ref, dn_ref,
    grad_ref,
):
    member = at_ref[1]
    masks = [
        jnp.concatenate(
            [causal_mask(member, others, late) for others in ((0, 1), (2, 3))], axis=0
        )
        for late in (False, True)
    ]
    pieces = ((own_ref, core_ref), (x_ref, far_ref))

    def both(block, columns):
        return jnp.concatenate([block_rows(refs, block, columns) for refs in pieces], axis=0)

    def project(phi, grad, rows, exact):
        back = features_back(phi, grad)
        if not exact:
            return dot(back.astype(BF16), rows)
        product = dot(jnp.concatenate(split(back), axis=0), rows)
        return product[:FD] + product[FD:]

    span = range(BLOCKS)
    values = [both(b, VALUE) for b in span]
    keys = [both(b, KEY) for b in span]
    queries = [block_rows((rows_ref,), b, QUERY) for b in span]
    phi_q = [phiq_ref[b] for b in span]
    phi_q16 = [p.astype(BF16) for p in phi_q]
    phi_k = [jnp.concatenate([phik_ref[b], phik2_ref[b]], axis=1) for b in span]
    grads = [dn_ref[b] for b in span]
    pairs = []
    for b in span:
        d_den = grads[b][HD:HD + 1].astype(F32) + grads[b][HD + 1:HD + 2].astype(F32)
        pair = dot(values[b], grads[b][:HD]) + d_den
        pairs.append(jnp.where(masks[b // 2], pair, 0.0).astype(BF16))
    terms = [dot(phi_q16[b], grads[b], NT) if b > 0 else None for b in span]
    later = [None] * BLOCKS
    total = terms[3]
    for b in (2, 1, 0):
        later[b] = total
        if b > 0:
            total = total + terms[b]
    grad_phi_q = []
    for b in span:
        if b == 0:
            both_terms = dot(jnp.concatenate(split(phi_k[b]), axis=0), pairs[b])
            grad_phi_q.append(both_terms[:PHI] + both_terms[PHI:])
        else:
            prior = prior_ref[b].T
            grad_phi_q.append(
                dot(phi_k[b].astype(BF16), pairs[b]) + dot(prior.astype(BF16), grads[b])
            )
    grad_phi_k = []
    for b in span:
        if b == BLOCKS - 1:
            grad_phi_k.append(dot(phi_q16[b], pairs[b], NT))
        else:
            grad = dot(
                jnp.concatenate([phi_q16[b], later[b][:, :HD].astype(BF16)], axis=1),
                jnp.concatenate([pairs[b], values[b]], axis=1),
                NT,
            )
            grad_phi_k.append(grad + (later[b][:, HD:HD + 1] + later[b][:, HD + 1:HD + 2]))
    grad_q = project(phi_q[0], grad_phi_q[0], queries[0], True)
    for b in range(1, BLOCKS):
        grad_q = grad_q + project(phi_q[b], grad_phi_q[b], queries[b], False)
    grad_k = project(phi_k[0], grad_phi_k[0], keys[0], True)
    for b in range(1, BLOCKS):
        grad_k = grad_k + project(phi_k[b], grad_phi_k[b], keys[b], False)
    odd = at_ref[1] % 2 == 1
    grad_ref[0] = jnp.where(odd, grad_k, grad_q)
    grad_ref[1] = jnp.where(odd, grad_q, grad_k)


def rest_kernel(
    at_ref, rows_ref, own_ref, core_ref, x_ref, far_ref, wk_ref, phiq_ref,
    top_ref, total_ref, acc_ref, num_ref, state_ref, phik_ref,
    student_ref, grad_ref,
    phik2_ref, prior_ref, dn_ref, *partial,
):
    second_kernel(
        at_ref, rows_ref, x_ref, far_ref, wk_ref, phiq_ref,
        top_ref, total_ref, acc_ref, num_ref, state_ref,
        student_ref, phik2_ref, prior_ref, dn_ref, *partial,
    )
    backward_kernel(
        at_ref, rows_ref, own_ref, core_ref, x_ref, far_ref, phiq_ref, phik_ref, phik2_ref,
        prior_ref, dn_ref, grad_ref,
    )


VMEM = pl.BlockSpec(memory_space=pltpu.VMEM)
SMEM = pl.BlockSpec(memory_space=pltpu.SMEM)
ANY = pl.BlockSpec(memory_space=pl.ANY)
PARAMS = pltpu.CompilerParams(vmem_limit_bytes=8 * 1024 * 1024)
PARTIAL = [
    ((BLOCKS, 1, ROWS), F32),
    ((BLOCKS, 1, ROWS), F32),
    ((BLOCKS, HD, ROWS), F32),
    ((BLOCKS, AUG, ROWS), F32),
    ((BLOCKS, AUG, PHI), F32),
]
PHI_KEYS = ((BLOCKS, PHI, HALF), F32)


def call(kernel, name, outs, args, scratch=(), flops=0, smem=True):
    return pl.pallas_call(
        kernel,
        out_shape=[jax.ShapeDtypeStruct(*out) for out in outs],
        in_specs=[SMEM if smem else VMEM] + [VMEM] * (len(args) - 1),
        out_specs=[VMEM] * len(outs),
        scratch_shapes=[pltpu.VMEM(*s) for s in scratch],
        compiler_params=PARAMS,
        cost_estimate=pl.CostEstimate(flops=flops, bytes_accessed=0, transcendentals=0),
        name=name,
    )(*args)


def tied(array, token):
    return pl.pallas_call(
        tie_kernel,
        out_shape=jax.ShapeDtypeStruct(array.shape, array.dtype),
        in_specs=[ANY, ANY],
        out_specs=ANY,
        input_output_aliases={0: 0},
        compiler_params=pltpu.CompilerParams(vmem_limit_bytes=1024 * 1024),
        name="tie",
    )(array, token)


def on_device(queries, keys, values, segment_ids, feat_query, feat_key):
    spot = lax.axis_index("ctx")
    place, member = spot // MEMBERS, spot % MEMBERS
    z_groups = [[j + MEMBERS * k for k in ORDER] for j in range(MEMBERS)]

    def swap(array, relative):
        return lax.ppermute(array, "ctx", [(i, i ^ relative) for i in range(32)])

    def along_z(array):
        return lax.all_to_all(array, "ctx", 0, 0, axis_index_groups=z_groups)

    at = jnp.stack([place, member]).astype(jnp.int32)

    sent, sent_q, flag = pl.pallas_call(
        pack_kernel,
        out_shape=[
            jax.ShapeDtypeStruct((PLACES, 2, SEG, 2 * HD), BF16),
            jax.ShapeDtypeStruct((PLACES, 2, SEG, HD), BF16),
            jax.ShapeDtypeStruct((1,), jnp.int32),
        ],
        in_specs=[ANY] * 4,
        out_specs=[VMEM, VMEM, SMEM],
        scratch_shapes=[
            pltpu.SMEM((2,), jnp.int32),
            pltpu.VMEM((2 * SEG * PLACES, HD), BF16),
            pltpu.VMEM((2 * SEG * PLACES, HD), F32),
            pltpu.VMEM((2 * SEG, HD), BF16),
            pltpu.VMEM((2 * SEG, HD), BF16),
            pltpu.SemaphoreType.DMA((4,)),
        ],
        compiler_params=pltpu.CompilerParams(vmem_limit_bytes=62 * 1024 * 1024),
        name="pack",
    )(
        segment_ids,
        queries.reshape(2 * SEG * PLACES, HD),
        keys.reshape(2 * SEG, HD),
        values.reshape(2 * SEG, HD),
    )
    own = along_z(sent)
    beside = swap(own, 2)
    core = swap(own, 1)
    rows = along_z(tied(sent_q, own))

    wq = jnp.transpose(feat_query, (0, 2, 1))
    wk = jnp.transpose(feat_key, (0, 2, 1))

    phi_q, *first = call(
        first_kernel, "first_half",
        [((BLOCKS, PHI, ROWS), F32)] + PARTIAL + [PHI_KEYS],
        (at, rows, own, core, wq, wk),
        flops=5 * 10 ** 9,
    )
    beside = tied(beside, rows)
    far = swap(beside, 1)
    student, grad = call(
        rest_kernel, "rest",
        [((PLACES, 2, SEG, HD), BF16), ((2, FD, HD), F32)],
        (at, rows, own, core, beside, far, wk, phi_q, *first),
        [PHI_KEYS, ((BLOCKS, AUG, PHI), F32), ((BLOCKS, AUG, ROWS), BF16)] + PARTIAL,
        flops=10 ** 10,
    )
    def swap_wide(array, relative):
        pairs = [(i, i ^ relative) for i in range(64)]
        return lax.ppermute(array, ("dp", "ctx"), pairs)

    (pair,) = call(
        pair_kernel, "pair", [((FD, HD), BF16)], (grad[0], swap(grad[1], 1)), smem=False
    )
    (share,) = call(
        share_kernel, "share", [((PLACES, 3, SEG, HD), BF16)],
        (pair, swap_wide(pair, 2), swap_wide(pair, 32), swap_wide(pair, 34), student),
        smem=False,
    )
    whole = along_z(share)
    other = swap(whole[:, 2], 1)
    (student,) = call(
        student_kernel, "student_rows", [((2 * SEG * PLACES, HD), BF16)], (flag, whole),
        [((2 * SEG * PLACES, HD), F32)],
    )
    student, grad_query, grad_key = call(
        finish_kernel, "finish",
        [((2 * SEG * PLACES, HD), BF16)] + [((PLACES, FD, HD), F32)] * 2,
        (at, student, whole, other),
    )
    student = student.reshape(2 * SEG, 1, PLACES, HD)
    return student, jnp.transpose(grad_query, (0, 2, 1)), jnp.transpose(grad_key, (0, 2, 1))


def solution(mesh):
    placed = (
        P("ctx", "dp", "tensor", None),
        P("ctx", "dp", "tensor", None),
        P("ctx", "dp", "tensor", None),
        P("ctx"),
        P("tensor", None, None),
        P("tensor", None, None),
    )
    return jax.shard_map(
        on_device,
        mesh=mesh,
        in_specs=placed,
        out_specs=(
            P("ctx", "dp", "tensor", None),
            P("tensor", None, None),
            P("tensor", None, None),
        ),
        check_vma=False,
    )
```
